32 devices in a mesh: space: 8 (over y, x, core), band: 4 (over z).
Axes of the slice: x: 2, y: 2, z: 4, core: 2. Of those that a mesh axis runs over, the one named last changes fastest.
Arguments:
- states: bfloat16 [82944, 1024], P('space', 'band'), may hold values from -12 to 12, as said below
- potential: float32 [82944], P('space'), may hold values from 0 to 2, as said below
- cell_matrix: bfloat16 [512, 512], replicated, may hold values from -1 to 1, as said below
- cell_scale: float32 [200], P('space'), may hold values from 0.5 to 1.5
- connectivity: int32 [200, 512], P('space'), may hold values from 0 to 10367, as said below
- lower_bound: float32 [1], replicated, may hold values from 0.4 to 0.8
- upper_bound: float32 [1], replicated, may hold values from 16 to 20
Outputs:
- filtered: bfloat16 [82944, 1024], P('space', 'band')
- projected: float32 [1024, 1024], P('band', 'space')
The draws below stay inside these ranges and needn't reach their ends.
Inputs may be any that keep to these rules, and one draw needn't show every extreme that they name: `connectivity`: each slab is a block of 5 x 5 x 1 hexahedral cells with 8 nodes along each edge, slabs stacked along the third dimension. Cell c of a slab is the cell at position (c % 5, (c // 5) % 5, c // 25), and its entry j is its node at corner offset (j % 8, (j // 8) % 8, j // 64). Nodes shared by cells get the same row. The nodes of node plane k along the third dimension have rows k * 1296 to (k + 1) * 1296 - 1 of the slab, in an order of their own. `states`: the copies of a node on a face shared by two slabs carry equal values. `potential`: the copies of a node on a face shared by two slabs carry equal values. `cell_matrix`: symmetric positive definite.
All inputs are finite; a program needn't handle non-finite values.
Results may differ from the reference program's by a relative error of at most 0.012.
The reference program's roundings to bfloat16 on the way count: a program that leaves them out, or rounds other values in their place, can miss the bound.
Values may be sent and summed in bfloat16 or wider, within the bound.
A program may use at most 128 MiB of HBM per device.

```python
import math
import jax
import jax.numpy as jnp
from jax import lax

EDGE = 8
STATES = 1024
SLAB_XY = 5
STEPS = 4
CELL_NODES = 512
FACE = 1296
LAYERS = 8
NODES_DEV = 10368
CELLS_DEV = 25
NODES = 82944
CELLS = 200
GLOBAL_NODES = 73872
N_SPACE = 8


def node_numbers(key):
    slab_count = NODES // NODES_DEV
    subkeys = jax.random.split(jax.random.fold_in(key, 4242), slab_count * LAYERS)
    within = jax.vmap(lambda subkey: jax.random.permutation(subkey, FACE))(subkeys).astype(jnp.int32)
    within = within.reshape(slab_count, LAYERS, FACE)
    planes = jnp.arange(LAYERS, dtype=jnp.int32)[None, :, None] * FACE
    return (planes + within).reshape(slab_count, NODES_DEV).astype(jnp.int32)


def face_lists(numbers):
    across = jnp.arange(FACE, dtype=jnp.int32)
    lower_ids = numbers[:, across]
    upper_ids = numbers[:, (LAYERS - 1) * FACE + across]
    return (lower_ids, upper_ids)


def pick_rows_drawn(slab_rows, face_ids):
    return slab_rows[face_ids]


def put_rows(slab_rows, face_ids, fresh_rows):
    return slab_rows.at[face_ids].set(fresh_rows)


def share_faces(values, numbers):
    lower_ids, upper_ids = face_lists(numbers)
    upper_rows = jax.vmap(pick_rows_drawn)(values, upper_ids)
    first_rows = jax.vmap(pick_rows_drawn)(values[:1], lower_ids[:1])
    source = jnp.concatenate([first_rows, upper_rows[:-1]], axis=0)
    return jax.vmap(put_rows)(values, lower_ids, source)


def draw_connectivity(key, part):
    numbers = node_numbers(key)
    side_nodes = (EDGE - 1) * SLAB_XY + 1
    corner = jnp.arange(EDGE, dtype=jnp.int32)
    cell_ids = jnp.arange(CELLS_DEV, dtype=jnp.int32)
    cell_x = cell_ids % SLAB_XY
    cell_y = cell_ids // SLAB_XY % SLAB_XY
    cell_z = cell_ids // (SLAB_XY * SLAB_XY)
    index_x = cell_x[:, None, None, None] * (EDGE - 1) + corner[None, None, None, :]
    index_y = cell_y[:, None, None, None] * (EDGE - 1) + corner[None, None, :, None]
    index_z = cell_z[:, None, None, None] * (EDGE - 1) + corner[None, :, None, None]
    drawn_rows = ((index_z * side_nodes + index_y) * side_nodes + index_x).reshape(CELLS_DEV, CELL_NODES)
    return numbers[:, drawn_rows].reshape(CELLS, CELL_NODES).astype(jnp.int32)


def draw_states(key, part):
    numbers = node_numbers(key)
    slab_count = NODES // NODES_DEV
    shape = (slab_count, NODES_DEV, STATES)
    plane = (jnp.arange(NODES_DEV, dtype=jnp.int32) // FACE).astype(jnp.float32) / (LAYERS - 1)
    rising = 0.4 * jnp.exp(jnp.log(6.0) * plane)
    values = jnp.clip(rising[None, :, None] * jax.random.normal(jax.random.fold_in(key, 11), shape, jnp.float32), -12.0, 12.0)
    values = share_faces(values, numbers)
    return values.reshape(NODES, STATES).astype(jnp.bfloat16)


def draw_potential(key, part):
    numbers = node_numbers(key)
    slab_count = NODES // NODES_DEV
    uniform_part = jax.random.uniform(jax.random.fold_in(key, 21), (slab_count, NODES_DEV, 1), jnp.float32, 0.0, 1.0)
    values = 2.0 * uniform_part
    values = share_faces(values, numbers)
    return values.reshape(NODES).astype(jnp.float32)


def draw_cell_matrix(key, part):
    factor = jax.random.normal(jax.random.fold_in(key, 32), (CELL_NODES, CELL_NODES), jnp.float32)
    gram = jnp.dot(factor, factor.T, precision=lax.Precision.HIGHEST) / (4.0 * CELL_NODES)
    return (gram + 0.1 * jnp.eye(CELL_NODES, dtype=jnp.float32)).astype(jnp.bfloat16)


def block_levels(rng, shape, shards, smallest, largest):
    factor_of = 1.0
    for position, parts in shards:
        heights = jax.random.uniform(jax.random.fold_in(jax.random.fold_in(rng, 6), position), (parts,), jnp.float32, smallest / len(shards), largest / len(shards))
        factor_of = factor_of * jnp.repeat(jnp.exp(heights), shape[position] // parts).reshape((-1,) + (1,) * (len(shape) - 1 - position))
    return factor_of


def setup_inputs(seed: int = 0) -> dict:
    seeds = jax.random.split(jax.random.key(seed), 8)
    return {
        "states": draw_states(jax.random.fold_in(seeds[7], 71), 0),
        "potential": draw_potential(jax.random.fold_in(seeds[7], 71), 0),
        "cell_matrix": draw_cell_matrix(jax.random.fold_in(seeds[7], 71), 0),
        "cell_scale": jnp.clip(jnp.exp(math.log(1.5) - 1.0986123 * jax.random.uniform(seeds[3], (CELLS,), jnp.float32) ** block_levels(seeds[3], (CELLS,), ((0, 8),), -0.2, 0.2)), 0.5, 1.5),
        "connectivity": draw_connectivity(jax.random.fold_in(seeds[7], 71), 0),
        "lower_bound": jnp.clip(jax.random.uniform(seeds[5], (1,), jnp.float32, 0.4, 0.8), 0.4, 0.8),
        "upper_bound": jnp.clip(jax.random.uniform(seeds[6], (1,), jnp.float32, 16.0, 20.0), 16.0, 20.0),
    }


def settle(values):
    return lax.optimization_barrier(values.astype(jnp.bfloat16))


def plain_index():
    side_nodes = (EDGE - 1) * SLAB_XY + 1
    corner = jnp.arange(EDGE, dtype=jnp.int32)
    cell_ids = jnp.arange(CELLS_DEV, dtype=jnp.int32)
    cell_x = cell_ids % SLAB_XY
    cell_y = (cell_ids // SLAB_XY) % SLAB_XY
    cell_z = cell_ids // (SLAB_XY * SLAB_XY)
    index_x = cell_x[:, None, None, None] * (EDGE - 1) + corner[None, None, None, :]
    index_y = cell_y[:, None, None, None] * (EDGE - 1) + corner[None, None, :, None]
    index_z = cell_z[:, None, None, None] * (EDGE - 1) + corner[None, :, None, None]
    return ((index_z * side_nodes + index_y) * side_nodes + index_x).reshape(CELLS_DEV, CELL_NODES).astype(jnp.int32)


def plane_rows(connect_slab):
    plain = plain_index()
    return jnp.zeros((NODES_DEV,), jnp.int32).at[plain.reshape(-1)].set(connect_slab.reshape(-1).astype(jnp.int32))


def slab_terms(values, connect_rows, scale_rows, matrix):
    gathered = values.astype(jnp.float32)[connect_rows]
    products = jnp.einsum("ij,cjs->cis", matrix, gathered, precision=lax.Precision.HIGHEST)
    products = products * scale_rows[:, None, None]
    return jax.ops.segment_sum(products.reshape(-1, STATES), connect_rows.reshape(-1), num_segments=NODES_DEV)


def pick_rows(slab_rows, face_ids):
    return slab_rows[face_ids]


def add_faces(slab_rows, low_ids, up_ids, add_low, add_up):
    return slab_rows.at[low_ids].add(add_low).at[up_ids].add(add_up)


def operator(stack, potential_rows, connect_all, scale_all, matrix, lower_ids, upper_ids):
    local = lax.map(lambda packed: slab_terms(packed[0], packed[1], packed[2], matrix), (stack, connect_all, scale_all))
    from_lower_faces = jax.vmap(pick_rows)(local, lower_ids)
    from_upper_faces = jax.vmap(pick_rows)(local, upper_ids)
    zero_face = jnp.zeros_like(from_upper_faces[:1])
    from_below = jnp.concatenate([zero_face, from_upper_faces[:-1]], axis=0)
    from_above = jnp.concatenate([from_lower_faces[1:], zero_face], axis=0)
    local = jax.vmap(add_faces)(local, lower_ids, upper_ids, from_below, from_above)
    return local + potential_rows[:, :, None] * stack.astype(jnp.float32)


def set_weights(weight_row, low_ids, up_ids, low_w, up_w):
    return weight_row.at[low_ids].set(low_w).at[up_ids].set(up_w)


def reference(states, potential, cell_matrix, cell_scale, connectivity, lower_bound, upper_bound):
    matrix = cell_matrix.astype(jnp.float32)
    stack = states.reshape(N_SPACE, NODES_DEV, STATES)
    potential_rows = potential.reshape(N_SPACE, NODES_DEV)
    connect_all = connectivity.reshape(N_SPACE, CELLS_DEV, CELL_NODES)
    scale_all = cell_scale.reshape(N_SPACE, CELLS_DEV)
    ordered = jax.vmap(plane_rows)(connect_all)
    lower_ids = ordered[:, :FACE]
    upper_ids = ordered[:, NODES_DEV - FACE:]
    center = (lower_bound[0] + upper_bound[0]) * 0.5
    half_width = (upper_bound[0] - lower_bound[0]) * 0.5

    def apply_h(values):
        return operator(values, potential_rows, connect_all, scale_all, matrix, lower_ids, upper_ids)

    previous = stack
    current = settle((apply_h(previous) - center * previous.astype(jnp.float32)) / half_width)
    for repeat in range(STEPS - 1):
        following = settle(2.0 * ((apply_h(current) - center * current.astype(jnp.float32)) / half_width) - previous.astype(jnp.float32))
        previous, current = current, following
    image = settle(apply_h(current))
    slab_index = jnp.arange(N_SPACE)
    lower_weight = jnp.where(slab_index > 0, 0.5, 1.0).astype(jnp.float32)
    upper_weight = jnp.where(slab_index < N_SPACE - 1, 0.5, 1.0).astype(jnp.float32)
    weights = jnp.ones((N_SPACE, NODES_DEV), jnp.float32)
    weights = jax.vmap(set_weights)(weights, lower_ids, upper_ids, lower_weight, upper_weight)
    weighted = settle(image.astype(jnp.float32) * weights[:, :, None])
    flat_states = current.reshape(-1, STATES).astype(jnp.float32)
    flat_images = weighted.reshape(-1, STATES).astype(jnp.float32)
    totals = lax.dot_general(flat_states, flat_images, (((0,), (0,)), ((), ())), precision=lax.Precision.HIGHEST)
    return current.reshape(NODES, STATES), totals / GLOBAL_NODES
```

```python
import functools

import jax
import jax.numpy as jnp
from jax import lax
from jax.experimental import pallas as pl
from jax.experimental.pallas import tpu as pltpu
from jax.sharding import PartitionSpec as P

EDGE = 8
SLAB_XY = 5
STEPS = 4
LANES = 128
SIDE = (EDGE - 1) * SLAB_XY + 1
FACE = SIDE * SIDE
CELLS = SLAB_XY * SLAB_XY
VMEM_BYTES = 58 * 1024 * 1024


def grid_order(connectivity):
    cells = connectivity.reshape(SLAB_XY, SLAB_XY, EDGE, EDGE, EDGE)
    main = cells[..., : EDGE - 1].transpose(2, 0, 3, 1, 4)
    main = main.reshape(EDGE, SLAB_XY, EDGE, SLAB_XY * (EDGE - 1))
    last = cells[:, SLAB_XY - 1, :, :, EDGE - 1].transpose(1, 0, 2)[..., None]
    rows = jnp.concatenate([main, last], axis=3)
    top = rows[:, :, : EDGE - 1].reshape(EDGE, SIDE - 1, SIDE)
    return jnp.concatenate([top, rows[:, SLAB_XY - 1, EDGE - 1 :]], axis=1).reshape(EDGE, FACE)


def sort_kernel(order_ref, states_ref, potential_ref, u_ref, pot_ref):
    z = pl.program_id(0)
    lane = lax.broadcasted_iota(jnp.int32, (FACE, EDGE), 1)
    column = jnp.sum(jnp.where(lane == z, order_ref[...], 0), axis=1, keepdims=True)
    hit = lax.broadcasted_iota(jnp.int32, (FACE, FACE), 1) == column
    picked = jnp.sum(jnp.where(hit, potential_ref[pl.ds(z, 1), :], 0.0), axis=1, keepdims=True)
    pot_ref[pl.ds(z, FACE, stride=EDGE), :] = jnp.broadcast_to(picked, (FACE, LANES))
    one_hot = jnp.where(hit, 1.0, 0.0).astype(jnp.bfloat16)
    rows = jnp.dot(one_hot, states_ref[...], preferred_element_type=jnp.float32)
    for h in range(u_ref.shape[0]):
        u_ref.at[h][pl.ds(z, FACE, stride=EDGE), :] = rows[:, h * LANES : (h + 1) * LANES]


def unsort_kernel(order_ref, f_ref, out_ref, wide):
    z = pl.program_id(0)
    halves = f_ref.shape[0]

    @pl.when(z == 0)
    def _():
        for h in range(halves):
            wide[h] = f_ref[h].astype(jnp.float32)

    row = order_ref[pl.ds(z, 1), :]
    hit = lax.broadcasted_iota(jnp.int32, (FACE, FACE), 0) == row
    one_hot = jnp.where(hit, 1.0, 0.0).astype(jnp.bfloat16)
    plane = jnp.concatenate(
        [wide.at[h][pl.ds(z, FACE, stride=EDGE), :] for h in range(halves)], axis=1
    ).astype(jnp.bfloat16)
    out_ref[...] = jnp.dot(one_hot, plane, preferred_element_type=jnp.float32).astype(jnp.bfloat16)


def filter_kernel(
    count, bounds_ref, scale_ref, u_hbm, pot_ref, matrix_ref, f_ref, w_ref,
    even, odd, acc, send, recv, load_sem, send_sem, recv_sem,
):
    halves = acc.shape[0]
    nodes = acc.shape[1]
    me = lax.axis_index("space")
    has_low = me > 0
    has_up = me < count - 1
    barrier = pltpu.get_barrier_semaphore()

    def greet(there, other):
        @pl.when(there)
        def _():
            pl.semaphore_signal(
                barrier, inc=1, device_id={"space": other}, device_id_type=pl.DeviceIdType.MESH
            )

    load = pltpu.make_async_copy(u_hbm, even, load_sem)
    load.start()
    greet(has_low, me - 1)
    greet(has_up, me + 1)
    pl.semaphore_wait(barrier, jnp.where(has_low, 1, 0) + jnp.where(has_up, 1, 0))
    load.wait()

    center = bounds_ref[0]
    inverse = bounds_ref[1]
    plane = lax.broadcasted_iota(jnp.int32, (EDGE, LANES), 0)
    low_w = jnp.where(has_low, 0.5, 1.0).astype(jnp.float32)
    up_w = jnp.where(has_up, 0.5, 1.0).astype(jnp.float32)
    weight = jnp.where(plane == 0, low_w, jnp.where(plane == EDGE - 1, up_w, 1.0))
    chunk = SIDE * EDGE
    weights = jnp.concatenate([weight] * SIDE, axis=0)

    def side_copy(step, h, side):
        return pltpu.make_async_remote_copy(
            src_ref=send.at[step % 2, h, side],
            dst_ref=recv.at[step % 2, h, 1 - side],
            send_sem=send_sem.at[step % 2, h, side],
            recv_sem=recv_sem.at[step % 2, h, 1 - side],
            device_id={"space": me - 1 if side == 0 else me + 1},
            device_id_type=pl.DeviceIdType.MESH,
        )

    def start_terms(u, h, shift):
        def body(i, carry):
            rows = pl.ds(pl.multiple_of(i * chunk, EDGE), chunk)
            acc[h, rows, :] = weights * (pot_ref[rows, :] - shift) * u[h, rows, :]
            return carry

        lax.fori_loop(0, SIDE, body, 0)

    def cell_rows(cell, y):
        corner = ((cell // SLAB_XY) * (EDGE - 1) + y) * SIDE + (cell % SLAB_XY) * (EDGE - 1)
        return pl.ds(pl.multiple_of(corner * EDGE, EDGE), EDGE * EDGE)

    def cells(u, h, group):
        blocks = [
            jnp.concatenate(
                [u[h, cell_rows(cell, y), :].astype(jnp.bfloat16) for y in range(EDGE)], axis=0
            )
            for cell in group
        ]
        block = blocks[0] if len(blocks) == 1 else jnp.concatenate(blocks, axis=1)
        product = jnp.dot(matrix_ref[...], block, preferred_element_type=jnp.float32)
        for place, cell in enumerate(group):
            scale = scale_ref[cell]
            for y in range(EDGE):
                part = product[y * EDGE * EDGE : (y + 1) * EDGE * EDGE, place * LANES : (place + 1) * LANES]
                acc[h, cell_rows(cell, y), :] += scale * part

    def all_cells(u, h):
        def body(i, carry):
            cells(u, h, (4 * i, 4 * i + 1))
            cells(u, h, (4 * i + 2, 4 * i + 3))
            return carry

        lax.fori_loop(0, CELLS // 4, body, 0)
        cells(u, h, (CELLS - 1,))

    def ship(step, h):
        for side, there in ((0, has_low), (1, has_up)):
            @pl.when(there)
            def _(side=side):
                rows = pl.ds(side * (EDGE - 1), FACE, stride=EDGE)
                send[step % 2, h, side] = acc.at[h][rows, :].astype(jnp.bfloat16)
                side_copy(step, h, side).start()

    def land(step, h):
        for side, there in ((0, has_low), (1, has_up)):
            @pl.when(there)
            def _(side=side):
                side_copy(step, h, side).wait_send()
                side_copy(step, h, 1 - side).wait_recv()
                rows = pl.ds(side * (EDGE - 1), FACE, stride=EDGE)
                acc.at[h][rows, :] = acc.at[h][rows, :] + recv[step % 2, h, side].astype(jnp.float32)

    def finish(step, h, fresh):
        shift = center if step < STEPS - 1 else 0.0

        def body(i, carry):
            rows = pl.ds(pl.multiple_of(i * chunk, EDGE), chunk)
            total = acc[h, rows, :] * inverse
            if step > 0:
                total = 2.0 * total - fresh[h, rows, :]
            narrow = total.astype(jnp.bfloat16)
            value = narrow.astype(jnp.float32)
            fresh[h, rows, :] = value
            acc[h, rows, :] = weights * (pot_ref[rows, :] - shift) * value
            return carry

        lax.fori_loop(0, SIDE, body, 0)
        if step == STEPS - 1:
            f_ref[h] = fresh[h].astype(jnp.bfloat16)

    fields = (even, odd)
    for h in range(halves):
        start_terms(even, h, center)
        all_cells(even, h)
        ship(0, h)
    for step in range(STEPS):
        fresh = fields[(step + 1) % 2]
        for h in range(halves):
            land(step, h)
            finish(step, h, fresh)
            all_cells(fresh, h)
            if step < STEPS - 1:
                ship(step + 1, h)
            else:
                w_ref[h] = acc[h].astype(jnp.bfloat16)


def vmem():
    return pl.BlockSpec(memory_space=pltpu.VMEM)


def smem():
    return pl.BlockSpec(memory_space=pltpu.SMEM)


def local(mesh, states, potential, cell_matrix, cell_scale, connectivity, lower_bound, upper_bound):
    nodes, columns = states.shape
    halves = columns // LANES
    slabs = lax.axis_size("space")
    bands = lax.axis_size("band")
    cell_nodes = cell_matrix.shape[0]
    order = grid_order(connectivity) - jnp.arange(EDGE, dtype=jnp.int32)[:, None] * FACE
    center = (lower_bound + upper_bound) * 0.5
    half_width = (upper_bound - lower_bound) * 0.5
    bounds = jnp.concatenate([center, 1.0 / half_width])

    number = jnp.arange(cell_nodes, dtype=jnp.int32)
    turned = (number % EDGE) * EDGE * EDGE + number // EDGE
    turn = (turned[:, None] == number[None, :]).astype(jnp.bfloat16)
    matrix = jnp.dot(turn, cell_matrix, preferred_element_type=jnp.float32).astype(jnp.bfloat16)
    matrix = jnp.dot(matrix, turn.T, preferred_element_type=jnp.float32).astype(jnp.bfloat16)

    whole = lambda *shape: pl.BlockSpec(shape, lambda z: (0,) * len(shape))
    start, pot = pl.pallas_call(
        sort_kernel,
        grid=(EDGE,),
        in_specs=[
            whole(FACE, EDGE),
            pl.BlockSpec((FACE, columns), lambda z: (z, 0)),
            whole(EDGE, FACE),
        ],
        out_specs=[whole(halves, nodes, LANES), whole(nodes, LANES)],
        out_shape=[
            jax.ShapeDtypeStruct((halves, nodes, LANES), jnp.float32),
            jax.ShapeDtypeStruct((nodes, LANES), jnp.float32),
        ],
        compiler_params=pltpu.CompilerParams(vmem_limit_bytes=VMEM_BYTES),
        name="sort_rows",
    )(order.T, states, potential.reshape(EDGE, FACE))

    dma = pltpu.SemaphoreType.DMA
    field = pltpu.VMEM((halves, nodes, LANES), jnp.float32)
    faces = pltpu.VMEM((2, halves, 2, FACE, LANES), jnp.bfloat16)
    narrow = jax.ShapeDtypeStruct((halves, nodes, LANES), jnp.bfloat16)
    filtered, image = pl.pallas_call(
        functools.partial(filter_kernel, slabs),
        in_specs=[smem(), smem(), pl.BlockSpec(memory_space=pl.ANY), vmem(), vmem()],
        out_specs=[vmem(), vmem()],
        out_shape=[narrow, narrow],
        scratch_shapes=[
            field, field, field, faces, faces,
            dma, dma((2, halves, 2)), dma((2, halves, 2)),
        ],
        compiler_params=pltpu.CompilerParams(
            collective_id=1, has_side_effects=True, vmem_limit_bytes=VMEM_BYTES
        ),
        name="filter_states",
    )(bounds, cell_scale, start, pot, matrix)

    out = pl.pallas_call(
        unsort_kernel,
        grid=(EDGE,),
        in_specs=[whole(EDGE, FACE), whole(halves, nodes, LANES)],
        out_specs=pl.BlockSpec((FACE, columns), lambda z: (z, 0)),
        out_shape=jax.ShapeDtypeStruct((nodes, columns), jnp.bfloat16),
        scratch_shapes=[field],
        compiler_params=pltpu.CompilerParams(vmem_limit_bytes=VMEM_BYTES),
        name="unsort_rows",
    )(order, filtered)

    return out, project(filtered, image, slabs, bands)


def project(filtered, image, slabs, bands):
    columns = filtered.shape[0] * LANES
    position = lax.axis_index("space")
    band = lax.axis_index("band")
    swap = position % 2 == 1
    role = jnp.where(swap, bands - 1 - band, band)
    middle = bands // 2

    def move(array, pairs):
        perm = []
        for s in range(slabs):
            for a, b in pairs:
                if s % 2:
                    a, b = bands - 1 - a, bands - 1 - b
                perm.append((s * bands + a, s * bands + b))
        return lax.ppermute(array, ("space", "band"), perm)

    rows = [filtered]
    for hop in range(1, middle + 1):
        rows.append(move(rows[-1], [(a, a + 1) for a in range(hop - 1, middle)]))
    images = [image]
    for hop in range(1, bands - middle):
        images.append(move(images[-1], [(a, a - 1) for a in range(middle + 1, bands - hop + 1)]))

    def product(f, w):
        blocks = [
            [
                lax.dot_general(f[i], w[j], (((0,), (0,)), ((), ())), preferred_element_type=jnp.float32)
                for j in range(f.shape[0])
            ]
            for i in range(f.shape[0])
        ]
        return jnp.block(blocks).astype(jnp.bfloat16)

    zero = jnp.zeros((columns, columns), jnp.bfloat16)
    grid = [[zero] * bands for _ in range(bands)]
    for up, f in enumerate(rows):
        for down, w in enumerate(images):
            block = product(f, w)
            for r in range(bands):
                a, b = r - up, r + down
                if a < 0 or b >= bands or (down and r < middle) or (up and r > middle):
                    continue
                kept = jnp.where(role == r, block, 0)
                grid[a][b] = grid[a][b] + kept
                if a != b:
                    grid[b][a] = grid[b][a] + kept.T
    plain = jnp.block(grid)
    mirrored = jnp.block([row[::-1] for row in grid[::-1]])
    partial = jnp.where(swap, mirrored, plain)
    sums = lax.psum_scatter(partial, "space", scatter_dimension=1, tiled=True)
    totals = lax.psum_scatter(sums, "band", scatter_dimension=0, tiled=True).astype(jnp.float32)
    return totals / (FACE * ((EDGE - 1) * slabs + 1))


def solution(mesh):
    placed = (P("space", "band"), P("space"), P(), P("space"), P("space", None), P(), P())
    return jax.shard_map(
        functools.partial(local, mesh),
        mesh=mesh,
        in_specs=placed,
        out_specs=(P("space", "band"), P("band", "space")),
        check_vma=False,
    )
```

```python
import functools

import jax
import jax.numpy as jnp
from jax import lax
from jax.experimental import pallas as pl
from jax.experimental.pallas import tpu as pltpu
from jax.sharding import PartitionSpec as P

EDGE = 8
SLAB_XY = 5
STEPS = 4
LANES = 128
SIDE = (EDGE - 1) * SLAB_XY + 1
FACE = SIDE * SIDE
CELLS = SLAB_XY * SLAB_XY
VMEM_BYTES = 58 * 1024 * 1024


def grid_order(connectivity):
    cells = connectivity.reshape(SLAB_XY, SLAB_XY, EDGE, EDGE, EDGE)
    main = cells[..., : EDGE - 1].transpose(2, 0, 3, 1, 4)
    main = main.reshape(EDGE, SLAB_XY, EDGE, SLAB_XY * (EDGE - 1))
    last = cells[:, SLAB_XY - 1, :, :, EDGE - 1].transpose(1, 0, 2)[..., None]
    rows = jnp.concatenate([main, last], axis=3)
    top = rows[:, :, : EDGE - 1].reshape(EDGE, SIDE - 1, SIDE)
    return jnp.concatenate([top, rows[:, SLAB_XY - 1, EDGE - 1 :]], axis=1).reshape(EDGE, FACE)


def sort_kernel(order_ref, states_ref, potential_ref, u_ref, pot_ref):
    z = pl.program_id(0)
    lane = lax.broadcasted_iota(jnp.int32, (FACE, EDGE), 1)
    column = jnp.sum(jnp.where(lane == z, order_ref[...], 0), axis=1, keepdims=True)
    hit = lax.broadcasted_iota(jnp.int32, (FACE, FACE), 1) == column
    picked = jnp.sum(jnp.where(hit, potential_ref[pl.ds(z, 1), :], 0.0), axis=1, keepdims=True)
    pot_ref[pl.ds(z, FACE, stride=EDGE), :] = jnp.broadcast_to(picked, (FACE, LANES))
    one_hot = jnp.where(hit, 1.0, 0.0).astype(jnp.bfloat16)
    rows = jnp.dot(one_hot, states_ref[...], preferred_element_type=jnp.float32)
    for h in range(u_ref.shape[0]):
        u_ref.at[h][pl.ds(z, FACE, stride=EDGE), :] = rows[:, h * LANES : (h + 1) * LANES]


def unsort_kernel(order_ref, f_ref, out_ref, wide):
    z = pl.program_id(0)
    halves = wide.shape[0]

    @pl.when(z == 0)
    def _():
        for h in range(halves):
            wide[h] = f_ref[:, h * LANES : (h + 1) * LANES].astype(jnp.float32)

    row = order_ref[pl.ds(z, 1), :]
    hit = lax.broadcasted_iota(jnp.int32, (FACE, FACE), 0) == row
    one_hot = jnp.where(hit, 1.0, 0.0).astype(jnp.bfloat16)
    plane = jnp.concatenate(
        [wide.at[h][pl.ds(z, FACE, stride=EDGE), :] for h in range(halves)], axis=1
    ).astype(jnp.bfloat16)
    out_ref[...] = jnp.dot(one_hot, plane, preferred_element_type=jnp.float32).astype(jnp.bfloat16)


def filter_kernel(
    count, bounds_ref, scale_ref, u_hbm, pot_ref, matrix_ref, f_ref, w_ref,
    even, odd, acc, send, recv, load_sem, send_sem, recv_sem,
):
    halves = acc.shape[0]
    nodes = acc.shape[1]
    me = lax.axis_index("space")
    has_low = me > 0
    has_up = me < count - 1
    barrier = pltpu.get_barrier_semaphore()

    def greet(there, other):
        @pl.when(there)
        def _():
            pl.semaphore_signal(
                barrier, inc=1, device_id={"space": other}, device_id_type=pl.DeviceIdType.MESH
            )

    load = pltpu.make_async_copy(u_hbm, even, load_sem)
    load.start()
    greet(has_low, me - 1)
    greet(has_up, me + 1)
    pl.semaphore_wait(barrier, jnp.where(has_low, 1, 0) + jnp.where(has_up, 1, 0))
    load.wait()

    center = bounds_ref[0]
    inverse = bounds_ref[1]
    plane = lax.broadcasted_iota(jnp.int32, (EDGE, LANES), 0)
    low_w = jnp.where(has_low, 0.5, 1.0).astype(jnp.float32)
    up_w = jnp.where(has_up, 0.5, 1.0).astype(jnp.float32)
    weight = jnp.where(plane == 0, low_w, jnp.where(plane == EDGE - 1, up_w, 1.0))
    chunk = SIDE * EDGE
    weights = jnp.concatenate([weight] * SIDE, axis=0)

    def side_copy(step, h, side):
        return pltpu.make_async_remote_copy(
            src_ref=send.at[step % 2, h, side],
            dst_ref=recv.at[step % 2, h, 1 - side],
            send_sem=send_sem.at[step % 2, h, side],
            recv_sem=recv_sem.at[step % 2, h, 1 - side],
            device_id={"space": me - 1 if side == 0 else me + 1},
            device_id_type=pl.DeviceIdType.MESH,
        )

    def start_terms(u, h, shift):
        def body(i, carry):
            rows = pl.ds(pl.multiple_of(i * chunk, EDGE), chunk)
            acc[h, rows, :] = weights * (pot_ref[rows, :] - shift) * u[h, rows, :]
            return carry

        lax.fori_loop(0, SIDE, body, 0)

    def cell_rows(cell, y):
        corner = ((cell // SLAB_XY) * (EDGE - 1) + y) * SIDE + (cell % SLAB_XY) * (EDGE - 1)
        return pl.ds(pl.multiple_of(corner * EDGE, EDGE), EDGE * EDGE)

    def cells(u, h, group):
        blocks = [
            jnp.concatenate(
                [u[h, cell_rows(cell, y), :].astype(jnp.bfloat16) for y in range(EDGE)], axis=0
            )
            for cell in group
        ]
        block = blocks[0] if len(blocks) == 1 else jnp.concatenate(blocks, axis=1)
        product = jnp.dot(matrix_ref[...], block, preferred_element_type=jnp.float32)
        for place, cell in enumerate(group):
            scale = scale_ref[cell]
            for y in range(EDGE):
                part = product[y * EDGE * EDGE : (y + 1) * EDGE * EDGE, place * LANES : (place + 1) * LANES]
                acc[h, cell_rows(cell, y), :] += scale * part

    def all_cells(u, h):
        def body(i, carry):
            cells(u, h, (4 * i, 4 * i + 1))
            cells(u, h, (4 * i + 2, 4 * i + 3))
            return carry

        lax.fori_loop(0, CELLS // 4, body, 0)
        cells(u, h, (CELLS - 1,))

    def ship(step, h):
        for side, there in ((0, has_low), (1, has_up)):
            @pl.when(there)
            def _(side=side):
                rows = pl.ds(side * (EDGE - 1), FACE, stride=EDGE)
                send[step % 2, h, side] = acc.at[h][rows, :].astype(jnp.bfloat16)
                side_copy(step, h, side).start()

    def land(step, h):
        for side, there in ((0, has_low), (1, has_up)):
            @pl.when(there)
            def _(side=side):
                side_copy(step, h, side).wait_send()
                side_copy(step, h, 1 - side).wait_recv()
                rows = pl.ds(side * (EDGE - 1), FACE, stride=EDGE)
                acc.at[h][rows, :] = acc.at[h][rows, :] + recv[step % 2, h, side].astype(jnp.float32)

    def finish(step, h, fresh):
        shift = center if step < STEPS - 1 else 0.0

        def body(i, carry):
            rows = pl.ds(pl.multiple_of(i * chunk, EDGE), chunk)
            total = acc[h, rows, :] * inverse
            if step > 0:
                total = 2.0 * total - fresh[h, rows, :]
            narrow = total.astype(jnp.bfloat16)
            value = narrow.astype(jnp.float32)
            fresh[h, rows, :] = value
            acc[h, rows, :] = weights * (pot_ref[rows, :] - shift) * value
            return carry

        lax.fori_loop(0, SIDE, body, 0)
        if step == STEPS - 1:
            f_ref[:, h * LANES : (h + 1) * LANES] = fresh[h].astype(jnp.bfloat16)

    fields = (even, odd)
    for h in range(halves):
        start_terms(even, h, center)
        all_cells(even, h)
        ship(0, h)
    for step in range(STEPS):
        fresh = fields[(step + 1) % 2]
        for h in range(halves):
            land(step, h)
            finish(step, h, fresh)
            all_cells(fresh, h)
            if step < STEPS - 1:
                ship(step + 1, h)
            else:
                w_ref[:, h * LANES : (h + 1) * LANES] = acc[h].astype(jnp.bfloat16)


def vmem():
    return pl.BlockSpec(memory_space=pltpu.VMEM)


def smem():
    return pl.BlockSpec(memory_space=pltpu.SMEM)


def local(mesh, states, potential, cell_matrix, cell_scale, connectivity, lower_bound, upper_bound):
    nodes, columns = states.shape
    halves = columns // LANES
    slabs = lax.axis_size("space")
    bands = lax.axis_size("band")
    cell_nodes = cell_matrix.shape[0]
    order = grid_order(connectivity) - jnp.arange(EDGE, dtype=jnp.int32)[:, None] * FACE
    center = (lower_bound + upper_bound) * 0.5
    half_width = (upper_bound - lower_bound) * 0.5
    bounds = jnp.concatenate([center, 1.0 / half_width])

    number = jnp.arange(cell_nodes, dtype=jnp.int32)
    turned = (number % EDGE) * EDGE * EDGE + number // EDGE
    turn = (turned[:, None] == number[None, :]).astype(jnp.bfloat16)
    matrix = jnp.dot(turn, cell_matrix, preferred_element_type=jnp.float32).astype(jnp.bfloat16)
    matrix = jnp.dot(matrix, turn.T, preferred_element_type=jnp.float32).astype(jnp.bfloat16)

    whole = lambda *shape: pl.BlockSpec(shape, lambda z: (0,) * len(shape))
    start, pot = pl.pallas_call(
        sort_kernel,
        grid=(EDGE,),
        in_specs=[
            whole(FACE, EDGE),
            pl.BlockSpec((FACE, columns), lambda z: (z, 0)),
            whole(EDGE, FACE),
        ],
        out_specs=[whole(halves, nodes, LANES), whole(nodes, LANES)],
        out_shape=[
            jax.ShapeDtypeStruct((halves, nodes, LANES), jnp.float32),
            jax.ShapeDtypeStruct((nodes, LANES), jnp.float32),
        ],
        compiler_params=pltpu.CompilerParams(vmem_limit_bytes=VMEM_BYTES),
        name="sort_rows",
    )(order.T, states, potential.reshape(EDGE, FACE))

    dma = pltpu.SemaphoreType.DMA
    field = pltpu.VMEM((halves, nodes, LANES), jnp.float32)
    faces = pltpu.VMEM((2, halves, 2, FACE, LANES), jnp.bfloat16)
    narrow = jax.ShapeDtypeStruct((nodes, columns), jnp.bfloat16)
    filtered, image = pl.pallas_call(
        functools.partial(filter_kernel, slabs),
        in_specs=[smem(), smem(), pl.BlockSpec(memory_space=pl.ANY), vmem(), vmem()],
        out_specs=[vmem(), vmem()],
        out_shape=[narrow, narrow],
        scratch_shapes=[
            field, field, field, faces, faces,
            dma, dma((2, halves, 2)), dma((2, halves, 2)),
        ],
        compiler_params=pltpu.CompilerParams(
            collective_id=1, has_side_effects=True, vmem_limit_bytes=VMEM_BYTES
        ),
        name="filter_states",
    )(bounds, cell_scale, start, pot, matrix)

    unsort = pl.pallas_call(
        unsort_kernel,
        grid=(EDGE,),
        in_specs=[whole(EDGE, FACE), whole(nodes, columns)],
        out_specs=pl.BlockSpec((FACE, columns), lambda z: (z, 0)),
        out_shape=jax.ShapeDtypeStruct((nodes, columns), jnp.bfloat16),
        scratch_shapes=[field],
        compiler_params=pltpu.CompilerParams(vmem_limit_bytes=VMEM_BYTES),
        cost_estimate=pl.CostEstimate(
            flops=2 * nodes * FACE * columns, bytes_accessed=4 * nodes * columns, transcendentals=0
        ),
        name="unsort_rows",
    )
    return project(filtered, image, slabs, bands, lambda: unsort(order, filtered))


def held_by(up, down, bands):
    middle = bands // 2
    first = middle if down else up
    last = middle if up else bands - 1 - down
    return first, last


def combine_kernel(slabs, bands, ups, downs, *refs):
    f_refs, w_refs = refs[:ups], refs[ups : ups + downs]
    out_ref, acc, whole, landed, send_sem, recv_sem = refs[ups + downs :]
    step = pl.program_id(0)
    width = acc.shape[-1]
    rows = whole.shape[0] // slabs
    me = lax.axis_index("space")
    band = lax.axis_index("band")
    swap = lax.rem(me, 2) == 1
    role = jnp.where(swap, bands - 1 - band, band)
    barrier = pltpu.get_barrier_semaphore()

    @pl.when(step == 0)
    def _():
        for d in range(1, slabs):
            pl.semaphore_signal(
                barrier,
                inc=1,
                device_id={"space": lax.rem(me + d, slabs)},
                device_id_type=pl.DeviceIdType.MESH,
            )
        acc[...] = jnp.zeros_like(acc)

    for up in range(ups):
        for down in range(downs):
            first, last = held_by(up, down, bands)

            @pl.when((role >= first) & (role <= last))
            def _(up=up, down=down):
                acc[up, down] += lax.dot_general(
                    f_refs[up][...],
                    w_refs[down][...],
                    (((0,), (0,)), ((), ())),
                    preferred_element_type=jnp.float32,
                )

    @pl.when(step == pl.num_programs(0) - 1)
    def _():
        whole[...] = jnp.zeros_like(whole)
        for mirrored in range(2):
            for up in range(ups):
                for down in range(downs):
                    first, last = held_by(up, down, bands)
                    for r in range(first, last + 1):
                        a, b = r - up, r + down
                        if mirrored:
                            a, b = bands - 1 - a, bands - 1 - b

                        @pl.when((role == r) & (swap if mirrored else jnp.logical_not(swap)))
                        def _(up=up, down=down, a=a, b=b):
                            block = acc[up, down]
                            whole[a * width : (a + 1) * width, b * width : (b + 1) * width] = block.astype(
                                jnp.bfloat16
                            )
                            if a != b:
                                whole[b * width : (b + 1) * width, a * width : (a + 1) * width] = (
                                    block.T.astype(jnp.bfloat16)
                                )

        pl.semaphore_wait(barrier, slabs - 1)
        copies = []
        for d in range(1, slabs):
            peer = lax.rem(me + d, slabs)
            copies.append(
                pltpu.make_async_remote_copy(
                    src_ref=whole.at[pl.ds(pl.multiple_of(peer * rows, rows), rows), :],
                    dst_ref=landed.at[d - 1],
                    send_sem=send_sem.at[d - 1],
                    recv_sem=recv_sem.at[d - 1],
                    device_id={"space": peer},
                    device_id_type=pl.DeviceIdType.MESH,
                )
            )
        for copy in copies:
            copy.start()
        total = whole[pl.ds(pl.multiple_of(me * rows, rows), rows), :].astype(jnp.float32)
        for d, copy in enumerate(copies):
            copy.wait_recv()
            total = total + landed[d].astype(jnp.float32)
        out_ref[...] = total.astype(jnp.bfloat16)
        for copy in copies:
            copy.wait_send()


def project(filtered, image, slabs, bands, unsort):
    nodes, columns = filtered.shape
    middle = bands // 2

    def move(array, pairs):
        perm = []
        for s in range(slabs):
            for a, b in pairs:
                if s % 2:
                    a, b = bands - 1 - a, bands - 1 - b
                perm.append((s * bands + a, s * bands + b))
        return lax.ppermute(array, ("space", "band"), perm)

    rows = [filtered, move(filtered, [(a, a + 1) for a in range(middle)])]
    out, rows[-1], image = lax.optimization_barrier((unsort(), rows[-1], image))
    for hop in range(2, middle + 1):
        rows.append(move(rows[-1], [(a, a + 1) for a in range(hop - 1, middle)]))
    images = [image]
    for hop in range(1, bands - middle):
        images.append(move(images[-1], [(a, a - 1) for a in range(middle + 1, bands - hop + 1)]))

    ups, downs = len(rows), len(images)
    states = bands * columns
    share = states // slabs
    dma = pltpu.SemaphoreType.DMA
    sums = pl.pallas_call(
        functools.partial(combine_kernel, slabs, bands, ups, downs),
        grid=(EDGE,),
        in_specs=[pl.BlockSpec((nodes // EDGE, columns), lambda z: (z, 0))] * (ups + downs),
        out_specs=pl.BlockSpec((share, states), lambda z: (0, 0)),
        out_shape=jax.ShapeDtypeStruct((share, states), jnp.bfloat16),
        scratch_shapes=[
            pltpu.VMEM((ups, downs, columns, columns), jnp.float32),
            pltpu.VMEM((states, states), jnp.bfloat16),
            pltpu.VMEM((slabs - 1, share, states), jnp.bfloat16),
            dma((slabs - 1,)),
            dma((slabs - 1,)),
        ],
        compiler_params=pltpu.CompilerParams(
            collective_id=2, has_side_effects=True, vmem_limit_bytes=VMEM_BYTES
        ),
        name="combine",
    )(*rows, *images)
    totals = lax.psum_scatter(sums, "band", scatter_dimension=1, tiled=True).astype(jnp.float32)
    return out, totals.T / (FACE * ((EDGE - 1) * slabs + 1))


def solution(mesh):
    placed = (P("space", "band"), P("space"), P(), P("space"), P("space", None), P(), P())
    return jax.shard_map(
        functools.partial(local, mesh),
        mesh=mesh,
        in_specs=placed,
        out_specs=(P("space", "band"), P("band", "space")),
        check_vma=False,
    )
```

```python
import functools

import jax
import jax.numpy as jnp
from jax import lax
from jax.experimental import pallas as pl
from jax.experimental.pallas import tpu as pltpu
from jax.sharding import PartitionSpec as P

EDGE = 8
SLAB_XY = 5
STEPS = 4
LANES = 128
SIDE = (EDGE - 1) * SLAB_XY + 1
FACE = SIDE * SIDE
CELLS = SLAB_XY * SLAB_XY
VMEM_BYTES = 58 * 1024 * 1024


def grid_order(connectivity):
    cells = connectivity.reshape(SLAB_XY, SLAB_XY, EDGE, EDGE, EDGE)
    main = cells[..., : EDGE - 1].transpose(2, 0, 3, 1, 4)
    main = main.reshape(EDGE, SLAB_XY, EDGE, SLAB_XY * (EDGE - 1))
    last = cells[:, SLAB_XY - 1, :, :, EDGE - 1].transpose(1, 0, 2)[..., None]
    rows = jnp.concatenate([main, last], axis=3)
    top = rows[:, :, : EDGE - 1].reshape(EDGE, SIDE - 1, SIDE)
    return jnp.concatenate([top, rows[:, SLAB_XY - 1, EDGE - 1 :]], axis=1).reshape(EDGE, FACE)


def sort_kernel(order_ref, states_ref, potential_ref, u_ref, pot_ref):
    z = pl.program_id(0)
    lane = lax.broadcasted_iota(jnp.int32, (FACE, EDGE), 1)
    column = jnp.sum(jnp.where(lane == z, order_ref[...], 0), axis=1, keepdims=True)
    hit = lax.broadcasted_iota(jnp.int32, (FACE, FACE), 1) == column
    picked = jnp.sum(jnp.where(hit, potential_ref[pl.ds(z, 1), :], 0.0), axis=1, keepdims=True)
    pot_ref[pl.ds(z, FACE, stride=EDGE), :] = jnp.broadcast_to(picked, (FACE, LANES))
    one_hot = jnp.where(hit, 1.0, 0.0).astype(jnp.bfloat16)
    rows = jnp.dot(one_hot, states_ref[...], preferred_element_type=jnp.float32)
    for h in range(u_ref.shape[0]):
        u_ref.at[h][pl.ds(z, FACE, stride=EDGE), :] = rows[:, h * LANES : (h + 1) * LANES]


def unsort_kernel(order_ref, f_ref, out_ref, wide):
    z = pl.program_id(0)
    halves = wide.shape[0]

    @pl.when(z == 0)
    def _():
        for h in range(halves):
            wide[h] = f_ref[:, h * LANES : (h + 1) * LANES].astype(jnp.float32)

    row = order_ref[pl.ds(z, 1), :]
    hit = lax.broadcasted_iota(jnp.int32, (FACE, FACE), 0) == row
    one_hot = jnp.where(hit, 1.0, 0.0).astype(jnp.bfloat16)
    plane = jnp.concatenate(
        [wide.at[h][pl.ds(z, FACE, stride=EDGE), :] for h in range(halves)], axis=1
    ).astype(jnp.bfloat16)
    out_ref[...] = jnp.dot(one_hot, plane, preferred_element_type=jnp.float32).astype(jnp.bfloat16)


def filter_kernel(
    count, bounds_ref, scale_ref, u_hbm, pot_ref, matrix_ref, f_ref, w_ref,
    even, odd, acc, send, recv, load_sem, send_sem, recv_sem,
):
    halves = acc.shape[0]
    nodes = acc.shape[1]
    me = lax.axis_index("space")
    has_low = me > 0
    has_up = me < count - 1
    barrier = pltpu.get_barrier_semaphore()

    def greet(there, other):
        @pl.when(there)
        def _():
            pl.semaphore_signal(
                barrier, inc=1, device_id={"space": other}, device_id_type=pl.DeviceIdType.MESH
            )

    load = pltpu.make_async_copy(u_hbm, even, load_sem)
    load.start()
    greet(has_low, me - 1)
    greet(has_up, me + 1)
    pl.semaphore_wait(barrier, jnp.where(has_low, 1, 0) + jnp.where(has_up, 1, 0))
    load.wait()

    center = bounds_ref[0]
    inverse = bounds_ref[1]
    plane = lax.broadcasted_iota(jnp.int32, (EDGE, LANES), 0)
    low_w = jnp.where(has_low, 0.5, 1.0).astype(jnp.float32)
    up_w = jnp.where(has_up, 0.5, 1.0).astype(jnp.float32)
    weight = jnp.where(plane == 0, low_w, jnp.where(plane == EDGE - 1, up_w, 1.0))
    chunk = SIDE * EDGE
    weights = jnp.concatenate([weight] * SIDE, axis=0)

    def side_copy(step, h, side):
        return pltpu.make_async_remote_copy(
            src_ref=send.at[step % 2, h, side],
            dst_ref=recv.at[step % 2, h, 1 - side],
            send_sem=send_sem.at[step % 2, h, side],
            recv_sem=recv_sem.at[step % 2, h, 1 - side],
            device_id={"space": me - 1 if side == 0 else me + 1},
            device_id_type=pl.DeviceIdType.MESH,
        )

    def start_terms(u, h, shift):
        def body(i, carry):
            rows = pl.ds(pl.multiple_of(i * chunk, EDGE), chunk)
            acc[h, rows, :] = weights * (pot_ref[rows, :] - shift) * u[h, rows, :]
            return carry

        lax.fori_loop(0, SIDE, body, 0)

    def cell_rows(cell, y):
        corner = ((cell // SLAB_XY) * (EDGE - 1) + y) * SIDE + (cell % SLAB_XY) * (EDGE - 1)
        return pl.ds(pl.multiple_of(corner * EDGE, EDGE), EDGE * EDGE)

    def cells(u, h, group):
        blocks = [
            jnp.concatenate(
                [u[h, cell_rows(cell, y), :].astype(jnp.bfloat16) for y in range(EDGE)], axis=0
            )
            for cell in group
        ]
        block = blocks[0] if len(blocks) == 1 else jnp.concatenate(blocks, axis=1)
        product = jnp.dot(matrix_ref[...], block, preferred_element_type=jnp.float32)
        for place, cell in enumerate(group):
            scale = scale_ref[cell]
            for y in range(EDGE):
                part = product[y * EDGE * EDGE : (y + 1) * EDGE * EDGE, place * LANES : (place + 1) * LANES]
                acc[h, cell_rows(cell, y), :] += scale * part

    def all_cells(u, h):
        def body(i, carry):
            cells(u, h, (4 * i, 4 * i + 1))
            cells(u, h, (4 * i + 2, 4 * i + 3))
            return carry

        lax.fori_loop(0, CELLS // 4, body, 0)
        cells(u, h, (CELLS - 1,))

    def ship(step, h):
        for side, there in ((0, has_low), (1, has_up)):
            @pl.when(there)
            def _(side=side):
                rows = pl.ds(side * (EDGE - 1), FACE, stride=EDGE)
                send[step % 2, h, side] = acc.at[h][rows, :].astype(jnp.bfloat16)
                side_copy(step, h, side).start()

    def land(step, h):
        for side, there in ((0, has_low), (1, has_up)):
            @pl.when(there)
            def _(side=side):
                side_copy(step, h, side).wait_send()
                side_copy(step, h, 1 - side).wait_recv()
                rows = pl.ds(side * (EDGE - 1), FACE, stride=EDGE)
                acc.at[h][rows, :] = acc.at[h][rows, :] + recv[step % 2, h, side].astype(jnp.float32)

    def finish(step, h, fresh):
        shift = center if step < STEPS - 1 else 0.0

        def body(i, carry):
            rows = pl.ds(pl.multiple_of(i * chunk, EDGE), chunk)
            total = acc[h, rows, :] * inverse
            if step > 0:
                total = 2.0 * total - fresh[h, rows, :]
            narrow = total.astype(jnp.bfloat16)
            value = narrow.astype(jnp.float32)
            fresh[h, rows, :] = value
            acc[h, rows, :] = weights * (pot_ref[rows, :] - shift) * value
            return carry

        lax.fori_loop(0, SIDE, body, 0)
        if step == STEPS - 1:
            f_ref[:, h * LANES : (h + 1) * LANES] = fresh[h].astype(jnp.bfloat16)

    fields = (even, odd)
    for h in range(halves):
        start_terms(even, h, center)
        all_cells(even, h)
        ship(0, h)
    for step in range(STEPS):
        fresh = fields[(step + 1) % 2]
        for h in range(halves):
            land(step, h)
            finish(step, h, fresh)
            all_cells(fresh, h)
            if step < STEPS - 1:
                ship(step + 1, h)
            else:
                w_ref[:, h * LANES : (h + 1) * LANES] = acc[h].astype(jnp.bfloat16)


def vmem():
    return pl.BlockSpec(memory_space=pltpu.VMEM)


def smem():
    return pl.BlockSpec(memory_space=pltpu.SMEM)


def local(mesh, states, potential, cell_matrix, cell_scale, connectivity, lower_bound, upper_bound):
    nodes, columns = states.shape
    halves = columns // LANES
    slabs = lax.axis_size("space")
    bands = lax.axis_size("band")
    cell_nodes = cell_matrix.shape[0]
    order = grid_order(connectivity) - jnp.arange(EDGE, dtype=jnp.int32)[:, None] * FACE
    center = (lower_bound + upper_bound) * 0.5
    half_width = (upper_bound - lower_bound) * 0.5
    bounds = jnp.concatenate([center, 1.0 / half_width])

    number = jnp.arange(cell_nodes, dtype=jnp.int32)
    turned = (number % EDGE) * EDGE * EDGE + number // EDGE
    turn = (turned[:, None] == number[None, :]).astype(jnp.bfloat16)
    matrix = jnp.dot(turn, cell_matrix, preferred_element_type=jnp.float32).astype(jnp.bfloat16)
    matrix = jnp.dot(matrix, turn.T, preferred_element_type=jnp.float32).astype(jnp.bfloat16)

    whole = lambda *shape: pl.BlockSpec(shape, lambda z: (0,) * len(shape))
    start, pot = pl.pallas_call(
        sort_kernel,
        grid=(EDGE,),
        in_specs=[
            whole(FACE, EDGE),
            pl.BlockSpec((FACE, columns), lambda z: (z, 0)),
            whole(EDGE, FACE),
        ],
        out_specs=[whole(halves, nodes, LANES), whole(nodes, LANES)],
        out_shape=[
            jax.ShapeDtypeStruct((halves, nodes, LANES), jnp.float32),
            jax.ShapeDtypeStruct((nodes, LANES), jnp.float32),
        ],
        compiler_params=pltpu.CompilerParams(vmem_limit_bytes=VMEM_BYTES),
        name="sort_rows",
    )(order.T, states, potential.reshape(EDGE, FACE))

    dma = pltpu.SemaphoreType.DMA
    field = pltpu.VMEM((halves, nodes, LANES), jnp.float32)
    faces = pltpu.VMEM((2, halves, 2, FACE, LANES), jnp.bfloat16)
    narrow = jax.ShapeDtypeStruct((nodes, columns), jnp.bfloat16)
    filtered, image = pl.pallas_call(
        functools.partial(filter_kernel, slabs),
        in_specs=[smem(), smem(), pl.BlockSpec(memory_space=pl.ANY), vmem(), vmem()],
        out_specs=[vmem(), vmem()],
        out_shape=[narrow, narrow],
        scratch_shapes=[
            field, field, field, faces, faces,
            dma, dma((2, halves, 2)), dma((2, halves, 2)),
        ],
        compiler_params=pltpu.CompilerParams(
            collective_id=1, has_side_effects=True, vmem_limit_bytes=VMEM_BYTES
        ),
        name="filter_states",
    )(bounds, cell_scale, start, pot, matrix)

    unsort = pl.pallas_call(
        unsort_kernel,
        grid=(EDGE,),
        in_specs=[whole(EDGE, FACE), whole(nodes, columns)],
        out_specs=pl.BlockSpec((FACE, columns), lambda z: (z, 0)),
        out_shape=jax.ShapeDtypeStruct((nodes, columns), jnp.bfloat16),
        scratch_shapes=[field],
        compiler_params=pltpu.CompilerParams(vmem_limit_bytes=VMEM_BYTES),
        cost_estimate=pl.CostEstimate(
            flops=2 * nodes * FACE * columns, bytes_accessed=4 * nodes * columns, transcendentals=0
        ),
        name="unsort_rows",
    )
    return project(filtered, image, slabs, bands, lambda: unsort(order, filtered))


def held_by(up, down, bands):
    middle = bands // 2
    first = middle if down else up
    last = middle if up else bands - 1 - down
    return first, last


def combine_kernel(slabs, bands, ups, downs, nodes_all, *refs):
    f_refs, w_refs = refs[:ups], refs[ups : ups + downs]
    out_ref, acc, whole, landed, mine, got, send_sem, recv_sem, band_send, band_recv = refs[ups + downs :]
    step = pl.program_id(0)
    width = acc.shape[1]
    rows = whole.shape[0] // slabs
    me = lax.axis_index("space")
    band = lax.axis_index("band")
    swap = lax.rem(me, 2) == 1
    role = jnp.where(swap, bands - 1 - band, band)
    barrier = pltpu.get_barrier_semaphore()

    @pl.when(step == 0)
    def _():
        for axis, place, count in (("space", me, slabs), ("band", band, bands)):
            for d in range(1, count):
                pl.semaphore_signal(
                    barrier,
                    inc=1,
                    device_id={axis: lax.rem(place + d, count)},
                    device_id_type=pl.DeviceIdType.MESH,
                )
        acc[...] = jnp.zeros_like(acc)

    held = {}
    for r in range(bands):
        for up in range(ups):
            for down in range(downs):
                first, last = held_by(up, down, bands)
                if first <= r <= last:
                    held.setdefault(r, {}).setdefault(down, []).append(up)

    for r, images in held.items():
        @pl.when(role == r)
        def _(images=images):
            for down, fields in images.items():
                sides = [f_refs[up][...] for up in fields]
                side = sides[0] if len(sides) == 1 else jnp.concatenate(sides, axis=1)
                acc[down, :, : len(fields) * width] += lax.dot_general(
                    w_refs[down][...], side, (((0,), (0,)), ((), ())), preferred_element_type=jnp.float32
                )

    @pl.when(step == pl.num_programs(0) - 1)
    def _():
        whole[...] = jnp.zeros_like(whole)
        for mirrored in range(2):
            for r, images in held.items():
                @pl.when((role == r) & (swap if mirrored else jnp.logical_not(swap)))
                def _(mirrored=mirrored, r=r, images=images):
                    for down, fields in images.items():
                        for up in fields:
                            a, b = r - up, r + down
                            if mirrored:
                                a, b = bands - 1 - a, bands - 1 - b
                            block = acc[down, :, up * width : (up + 1) * width]
                            across, along = pl.ds(b * width, width), pl.ds(a * width, width)
                            whole[across, along] = block.astype(jnp.bfloat16)
                            if a != b:
                                whole[along, across] = block.T.astype(jnp.bfloat16)

        pl.semaphore_wait(barrier, slabs - 1 + bands - 1)
        copies = []
        for d in range(1, slabs):
            peer = lax.rem(me + d, slabs)
            copies.append(
                pltpu.make_async_remote_copy(
                    src_ref=whole.at[pl.ds(pl.multiple_of(peer * rows, rows), rows), :],
                    dst_ref=landed.at[d - 1],
                    send_sem=send_sem.at[d - 1],
                    recv_sem=recv_sem.at[d - 1],
                    device_id={"space": peer},
                    device_id_type=pl.DeviceIdType.MESH,
                )
            )
        for copy in copies:
            copy.start()
        total = whole[pl.ds(pl.multiple_of(me * rows, rows), rows), :].astype(jnp.float32)
        for d, copy in enumerate(copies):
            copy.wait_recv()
            total = total + landed[d].astype(jnp.float32)
        for q in range(bands):
            mine[q] = total[:, q * width : (q + 1) * width].astype(jnp.bfloat16)
        across = []
        for d in range(1, bands):
            peer = lax.rem(band + d, bands)
            across.append(
                pltpu.make_async_remote_copy(
                    src_ref=mine.at[peer],
                    dst_ref=got.at[d - 1],
                    send_sem=band_send.at[d - 1],
                    recv_sem=band_recv.at[d - 1],
                    device_id={"band": peer},
                    device_id_type=pl.DeviceIdType.MESH,
                )
            )
        for copy in across:
            copy.start()
        total = mine[band].astype(jnp.float32)
        for d, copy in enumerate(across):
            copy.wait_recv()
            total = total + got[d].astype(jnp.float32)
        out_ref[...] = total.T / nodes_all
        for copy in copies + across:
            copy.wait_send()


def project(filtered, image, slabs, bands, unsort):
    nodes, columns = filtered.shape
    middle = bands // 2

    def move(array, pairs):
        perm = []
        for s in range(slabs):
            for a, b in pairs:
                if s % 2:
                    a, b = bands - 1 - a, bands - 1 - b
                perm.append((s * bands + a, s * bands + b))
        return lax.ppermute(array, ("space", "band"), perm)

    rows = [filtered, move(filtered, [(a, a + 1) for a in range(middle)])]
    out, rows[-1], image = lax.optimization_barrier((unsort(), rows[-1], image))
    for hop in range(2, middle + 1):
        rows.append(move(rows[-1], [(a, a + 1) for a in range(hop - 1, middle)]))
    images = [image]
    for hop in range(1, bands - middle):
        images.append(move(images[-1], [(a, a - 1) for a in range(middle + 1, bands - hop + 1)]))

    ups, downs = len(rows), len(images)
    states = bands * columns
    share = states // slabs
    dma = pltpu.SemaphoreType.DMA
    narrow = jnp.bfloat16
    projected = pl.pallas_call(
        functools.partial(
            combine_kernel, slabs, bands, ups, downs, FACE * ((EDGE - 1) * slabs + 1)
        ),
        grid=(EDGE,),
        in_specs=[pl.BlockSpec((nodes // EDGE, columns), lambda z: (z, 0))] * (ups + downs),
        out_specs=pl.BlockSpec((columns, share), lambda z: (0, 0)),
        out_shape=jax.ShapeDtypeStruct((columns, share), jnp.float32),
        scratch_shapes=[
            pltpu.VMEM((downs, columns, ups * columns), jnp.float32),
            pltpu.VMEM((states, states), narrow),
            pltpu.VMEM((slabs - 1, share, states), narrow),
            pltpu.VMEM((bands, share, columns), narrow),
            pltpu.VMEM((bands - 1, share, columns), narrow),
            dma((slabs - 1,)),
            dma((slabs - 1,)),
            dma((bands - 1,)),
            dma((bands - 1,)),
        ],
        compiler_params=pltpu.CompilerParams(
            collective_id=2, has_side_effects=True, vmem_limit_bytes=VMEM_BYTES
        ),
        name="combine",
    )(*rows, *images)
    return out, projected


def solution(mesh):
    placed = (P("space", "band"), P("space"), P(), P("space"), P("space", None), P(), P())
    return jax.shard_map(
        functools.partial(local, mesh),
        mesh=mesh,
        in_specs=placed,
        out_specs=(P("space", "band"), P("band", "space")),
        check_vma=False,
    )
```

```python
import functools

import jax
import jax.numpy as jnp
from jax import lax
from jax.experimental import pallas as pl
from jax.experimental.pallas import tpu as pltpu
from jax.sharding import PartitionSpec as P

EDGE = 8
SLAB_XY = 5
STEPS = 4
LANES = 128
SIDE = (EDGE - 1) * SLAB_XY + 1
FACE = SIDE * SIDE
CELLS = SLAB_XY * SLAB_XY
VMEM_BYTES = 58 * 1024 * 1024


def grid_order(connectivity):
    cells = connectivity.reshape(SLAB_XY, SLAB_XY, EDGE, EDGE, EDGE)
    main = cells[..., : EDGE - 1].transpose(2, 0, 3, 1, 4)
    main = main.reshape(EDGE, SLAB_XY, EDGE, SLAB_XY * (EDGE - 1))
    last = cells[:, SLAB_XY - 1, :, :, EDGE - 1].transpose(1, 0, 2)[..., None]
    rows = jnp.concatenate([main, last], axis=3)
    top = rows[:, :, : EDGE - 1].reshape(EDGE, SIDE - 1, SIDE)
    return jnp.concatenate([top, rows[:, SLAB_XY - 1, EDGE - 1 :]], axis=1).reshape(EDGE, FACE)


def sort_kernel(order_ref, states_ref, potential_ref, u_ref, pot_ref):
    z = pl.program_id(0)
    lane = lax.broadcasted_iota(jnp.int32, (FACE, EDGE), 1)
    column = jnp.sum(jnp.where(lane == z, order_ref[...], 0), axis=1, keepdims=True)
    hit = lax.broadcasted_iota(jnp.int32, (FACE, FACE), 1) == column
    picked = jnp.sum(jnp.where(hit, potential_ref[pl.ds(z, 1), :], 0.0), axis=1, keepdims=True)
    pot_ref[pl.ds(z, FACE, stride=EDGE), :] = jnp.broadcast_to(picked, (FACE, LANES))
    one_hot = jnp.where(hit, 1.0, 0.0).astype(jnp.bfloat16)
    rows = jnp.dot(one_hot, states_ref[...], preferred_element_type=jnp.float32)
    for h in range(u_ref.shape[0]):
        u_ref.at[h][pl.ds(z, FACE, stride=EDGE), :] = rows[:, h * LANES : (h + 1) * LANES]


def unsort_kernel(order_ref, f_ref, out_ref, wide):
    z = pl.program_id(0)
    halves = wide.shape[0]

    @pl.when(z == 0)
    def _():
        for h in range(halves):
            wide[h] = f_ref[:, h * LANES : (h + 1) * LANES].astype(jnp.float32)

    row = order_ref[pl.ds(z, 1), :]
    hit = lax.broadcasted_iota(jnp.int32, (FACE, FACE), 0) == row
    one_hot = jnp.where(hit, 1.0, 0.0).astype(jnp.bfloat16)
    plane = jnp.concatenate(
        [wide.at[h][pl.ds(z, FACE, stride=EDGE), :] for h in range(halves)], axis=1
    ).astype(jnp.bfloat16)
    out_ref[...] = jnp.dot(one_hot, plane, preferred_element_type=jnp.float32).astype(jnp.bfloat16)


def filter_kernel(
    count, bands, bounds_ref, scale_ref, u_hbm, pot_ref, matrix_ref, f_ref, w_ref, next_hbm,
    even, odd, acc, send, recv, load_sem, send_sem, recv_sem, hop_send, hop_recv,
):
    halves = acc.shape[0]
    nodes = acc.shape[1]
    me = lax.axis_index("space")
    has_low = me > 0
    has_up = me < count - 1
    barrier = pltpu.get_barrier_semaphore()

    band = lax.axis_index("band")
    swap = lax.rem(me, 2) == 1
    role = jnp.where(swap, bands - 1 - band, band)
    onward = jnp.where(swap, -1, 1)
    gives = role < bands // 2
    takes = (role > 0) & (role <= bands // 2)

    def greet(there, axis, other):
        @pl.when(there)
        def _():
            pl.semaphore_signal(
                barrier, inc=1, device_id={axis: other}, device_id_type=pl.DeviceIdType.MESH
            )

    load = pltpu.make_async_copy(u_hbm, even, load_sem)
    load.start()
    peers = (
        (has_low, "space", me - 1),
        (has_up, "space", me + 1),
        (gives, "band", band + onward),
        (takes, "band", band - onward),
    )
    for peer in peers:
        greet(*peer)
    pl.semaphore_wait(barrier, sum(jnp.where(peer[0], 1, 0) for peer in peers))
    load.wait()

    center = bounds_ref[0]
    inverse = bounds_ref[1]
    plane = lax.broadcasted_iota(jnp.int32, (EDGE, LANES), 0)
    low_w = jnp.where(has_low, 0.5, 1.0).astype(jnp.float32)
    up_w = jnp.where(has_up, 0.5, 1.0).astype(jnp.float32)
    weight = jnp.where(plane == 0, low_w, jnp.where(plane == EDGE - 1, up_w, 1.0))
    chunk = SIDE * EDGE
    weights = jnp.concatenate([weight] * SIDE, axis=0)

    def side_copy(step, h, side):
        return pltpu.make_async_remote_copy(
            src_ref=send.at[step % 2, h, side],
            dst_ref=recv.at[step % 2, h, 1 - side],
            send_sem=send_sem.at[step % 2, h, side],
            recv_sem=recv_sem.at[step % 2, h, 1 - side],
            device_id={"space": me - 1 if side == 0 else me + 1},
            device_id_type=pl.DeviceIdType.MESH,
        )

    def hop(h):
        part = pl.ds(h * LANES, LANES)
        return pltpu.make_async_remote_copy(
            src_ref=f_ref.at[:, part],
            dst_ref=next_hbm.at[:, part],
            send_sem=hop_send.at[h],
            recv_sem=hop_recv.at[h],
            device_id={"band": band + onward},
            device_id_type=pl.DeviceIdType.MESH,
        )

    def start_terms(u, h, shift):
        def body(i, carry):
            rows = pl.ds(pl.multiple_of(i * chunk, EDGE), chunk)
            acc[h, rows, :] = weights * (pot_ref[rows, :] - shift) * u[h, rows, :]
            return carry

        lax.fori_loop(0, SIDE, body, 0)

    def cell_rows(cell, y):
        corner = ((cell // SLAB_XY) * (EDGE - 1) + y) * SIDE + (cell % SLAB_XY) * (EDGE - 1)
        return pl.ds(pl.multiple_of(corner * EDGE, EDGE), EDGE * EDGE)

    def cells(u, h, group):
        blocks = [
            jnp.concatenate(
                [u[h, cell_rows(cell, y), :].astype(jnp.bfloat16) for y in range(EDGE)], axis=0
            )
            for cell in group
        ]
        block = blocks[0] if len(blocks) == 1 else jnp.concatenate(blocks, axis=1)
        product = jnp.dot(matrix_ref[...], block, preferred_element_type=jnp.float32)
        for place, cell in enumerate(group):
            scale = scale_ref[cell]
            for y in range(EDGE):
                part = product[y * EDGE * EDGE : (y + 1) * EDGE * EDGE, place * LANES : (place + 1) * LANES]
                acc[h, cell_rows(cell, y), :] += scale * part

    def all_cells(u, h):
        def body(i, carry):
            cells(u, h, (4 * i, 4 * i + 1))
            cells(u, h, (4 * i + 2, 4 * i + 3))
            return carry

        lax.fori_loop(0, CELLS // 4, body, 0)
        cells(u, h, (CELLS - 1,))

    def ship(step, h):
        for side, there in ((0, has_low), (1, has_up)):
            @pl.when(there)
            def _(side=side):
                rows = pl.ds(side * (EDGE - 1), FACE, stride=EDGE)
                send[step % 2, h, side] = acc.at[h][rows, :].astype(jnp.bfloat16)
                side_copy(step, h, side).start()

    def land(step, h):
        for side, there in ((0, has_low), (1, has_up)):
            @pl.when(there)
            def _(side=side):
                side_copy(step, h, side).wait_send()
                side_copy(step, h, 1 - side).wait_recv()
                rows = pl.ds(side * (EDGE - 1), FACE, stride=EDGE)
                acc.at[h][rows, :] = acc.at[h][rows, :] + recv[step % 2, h, side].astype(jnp.float32)

    def finish(step, h, fresh):
        shift = center if step < STEPS - 1 else 0.0

        def body(i, carry):
            rows = pl.ds(pl.multiple_of(i * chunk, EDGE), chunk)
            total = acc[h, rows, :] * inverse
            if step > 0:
                total = 2.0 * total - fresh[h, rows, :]
            narrow = total.astype(jnp.bfloat16)
            value = narrow.astype(jnp.float32)
            fresh[h, rows, :] = value
            acc[h, rows, :] = weights * (pot_ref[rows, :] - shift) * value
            return carry

        lax.fori_loop(0, SIDE, body, 0)
        if step == STEPS - 1:
            f_ref[:, h * LANES : (h + 1) * LANES] = fresh[h].astype(jnp.bfloat16)

            @pl.when(gives)
            def _():
                hop(h).start()

    fields = (even, odd)
    for h in range(halves):
        start_terms(even, h, center)
        all_cells(even, h)
        ship(0, h)
    for step in range(STEPS):
        fresh = fields[(step + 1) % 2]
        for h in range(halves):
            land(step, h)
            finish(step, h, fresh)
            all_cells(fresh, h)
            if step < STEPS - 1:
                ship(step + 1, h)
            else:
                w_ref[:, h * LANES : (h + 1) * LANES] = acc[h].astype(jnp.bfloat16)
    for h in range(halves):
        @pl.when(gives)
        def _(h=h):
            hop(h).wait_send()

        @pl.when(takes)
        def _(h=h):
            hop(h).wait_recv()


def vmem():
    return pl.BlockSpec(memory_space=pltpu.VMEM)


def smem():
    return pl.BlockSpec(memory_space=pltpu.SMEM)


def local(mesh, states, potential, cell_matrix, cell_scale, connectivity, lower_bound, upper_bound):
    nodes, columns = states.shape
    halves = columns // LANES
    slabs = lax.axis_size("space")
    bands = lax.axis_size("band")
    cell_nodes = cell_matrix.shape[0]
    order = grid_order(connectivity) - jnp.arange(EDGE, dtype=jnp.int32)[:, None] * FACE
    center = (lower_bound + upper_bound) * 0.5
    half_width = (upper_bound - lower_bound) * 0.5
    bounds = jnp.concatenate([center, 1.0 / half_width])

    number = jnp.arange(cell_nodes, dtype=jnp.int32)
    turned = (number % EDGE) * EDGE * EDGE + number // EDGE
    turn = (turned[:, None] == number[None, :]).astype(jnp.bfloat16)
    matrix = jnp.dot(turn, cell_matrix, preferred_element_type=jnp.float32).astype(jnp.bfloat16)
    matrix = jnp.dot(matrix, turn.T, preferred_element_type=jnp.float32).astype(jnp.bfloat16)

    whole = lambda *shape: pl.BlockSpec(shape, lambda z: (0,) * len(shape))
    start, pot = pl.pallas_call(
        sort_kernel,
        grid=(EDGE,),
        in_specs=[
            whole(FACE, EDGE),
            pl.BlockSpec((FACE, columns), lambda z: (z, 0)),
            whole(EDGE, FACE),
        ],
        out_specs=[whole(halves, nodes, LANES), whole(nodes, LANES)],
        out_shape=[
            jax.ShapeDtypeStruct((halves, nodes, LANES), jnp.float32),
            jax.ShapeDtypeStruct((nodes, LANES), jnp.float32),
        ],
        compiler_params=pltpu.CompilerParams(vmem_limit_bytes=VMEM_BYTES),
        name="sort_rows",
    )(order.T, states, potential.reshape(EDGE, FACE))

    dma = pltpu.SemaphoreType.DMA
    field = pltpu.VMEM((halves, nodes, LANES), jnp.float32)
    faces = pltpu.VMEM((2, halves, 2, FACE, LANES), jnp.bfloat16)
    narrow = jax.ShapeDtypeStruct((nodes, columns), jnp.bfloat16)
    filtered, image, landed = pl.pallas_call(
        functools.partial(filter_kernel, slabs, bands),
        in_specs=[smem(), smem(), pl.BlockSpec(memory_space=pl.ANY), vmem(), vmem()],
        out_specs=[vmem(), vmem(), pl.BlockSpec(memory_space=pl.ANY)],
        out_shape=[narrow, narrow, narrow],
        scratch_shapes=[
            field, field, field, faces, faces,
            dma, dma((2, halves, 2)), dma((2, halves, 2)), dma((halves,)), dma((halves,)),
        ],
        compiler_params=pltpu.CompilerParams(
            collective_id=1, has_side_effects=True, vmem_limit_bytes=VMEM_BYTES
        ),
        name="filter_states",
    )(bounds, cell_scale, start, pot, matrix)

    unsort = pl.pallas_call(
        unsort_kernel,
        grid=(EDGE,),
        in_specs=[whole(EDGE, FACE), whole(nodes, columns)],
        out_specs=pl.BlockSpec((FACE, columns), lambda z: (z, 0)),
        out_shape=jax.ShapeDtypeStruct((nodes, columns), jnp.bfloat16),
        scratch_shapes=[field],
        compiler_params=pltpu.CompilerParams(vmem_limit_bytes=VMEM_BYTES),
        cost_estimate=pl.CostEstimate(
            flops=2 * nodes * FACE * columns, bytes_accessed=4 * nodes * columns, transcendentals=0
        ),
        name="unsort_rows",
    )
    return unsort(order, filtered), project(filtered, landed, image, slabs, bands)


def held_by(up, down, bands):
    middle = bands // 2
    first = middle if down else up
    last = middle if up else bands - 1 - down
    return first, last


def early_kernel(f_ref, next_ref, w_ref, out_ref):
    @pl.when(pl.program_id(0) == 0)
    def _():
        out_ref[...] = jnp.zeros_like(out_ref)

    side = jnp.concatenate([f_ref[...], next_ref[...]], axis=1)
    out_ref[...] += lax.dot_general(
        w_ref[...], side, (((0,), (0,)), ((), ())), preferred_element_type=jnp.float32
    )


def combine_kernel(slabs, bands, ups, downs, nodes_all, *refs):
    f_refs, w_refs, early_ref = refs[:ups], refs[ups : ups + downs], refs[ups + downs]
    out_ref, acc, whole, landed, mine, got, send_sem, recv_sem, band_send, band_recv = refs[ups + downs + 1 :]
    step = pl.program_id(0)
    width = acc.shape[1]
    rows = whole.shape[0] // slabs
    me = lax.axis_index("space")
    band = lax.axis_index("band")
    swap = lax.rem(me, 2) == 1
    role = jnp.where(swap, bands - 1 - band, band)
    barrier = pltpu.get_barrier_semaphore()

    @pl.when(step == 0)
    def _():
        for axis, place, count in (("space", me, slabs), ("band", band, bands)):
            for d in range(1, count):
                pl.semaphore_signal(
                    barrier,
                    inc=1,
                    device_id={axis: lax.rem(place + d, count)},
                    device_id_type=pl.DeviceIdType.MESH,
                )
        acc[...] = jnp.zeros_like(acc)
        acc[0, :, : 2 * width] = early_ref[...]

    held = {}
    for r in range(bands):
        for up in range(ups):
            for down in range(downs):
                first, last = held_by(up, down, bands)
                if first <= r <= last:
                    held.setdefault(r, {}).setdefault(down, []).append(up)

    for r, images in held.items():
        @pl.when(role == r)
        def _(images=images):
            for down, fields in images.items():
                begin = 0 if down else 2
                fields = fields[begin:]
                if not fields:
                    continue
                sides = [f_refs[up][...] for up in fields]
                side = sides[0] if len(sides) == 1 else jnp.concatenate(sides, axis=1)
                acc[down, :, begin * width : (begin + len(fields)) * width] += lax.dot_general(
                    w_refs[down][...], side, (((0,), (0,)), ((), ())), preferred_element_type=jnp.float32
                )

    @pl.when(step == pl.num_programs(0) - 1)
    def _():
        whole[...] = jnp.zeros_like(whole)
        for mirrored in range(2):
            for r, images in held.items():
                @pl.when((role == r) & (swap if mirrored else jnp.logical_not(swap)))
                def _(mirrored=mirrored, r=r, images=images):
                    for down, fields in images.items():
                        for up in fields:
                            a, b = r - up, r + down
                            if mirrored:
                                a, b = bands - 1 - a, bands - 1 - b
                            block = acc[down, :, up * width : (up + 1) * width]
                            across, along = pl.ds(b * width, width), pl.ds(a * width, width)
                            whole[across, along] = block.astype(jnp.bfloat16)
                            if a != b:
                                whole[along, across] = block.T.astype(jnp.bfloat16)

        pl.semaphore_wait(barrier, slabs - 1 + bands - 1)
        copies = []
        for d in range(1, slabs):
            peer = lax.rem(me + d, slabs)
            copies.append(
                pltpu.make_async_remote_copy(
                    src_ref=whole.at[pl.ds(pl.multiple_of(peer * rows, rows), rows), :],
                    dst_ref=landed.at[d - 1],
                    send_sem=send_sem.at[d - 1],
                    recv_sem=recv_sem.at[d - 1],
                    device_id={"space": peer},
                    device_id_type=pl.DeviceIdType.MESH,
                )
            )
        for copy in copies:
            copy.start()
        total = whole[pl.ds(pl.multiple_of(me * rows, rows), rows), :].astype(jnp.float32)
        for d, copy in enumerate(copies):
            copy.wait_recv()
            total = total + landed[d].astype(jnp.float32)
        for q in range(bands):
            mine[q] = total[:, q * width : (q + 1) * width].astype(jnp.bfloat16)
        across = []
        for d in range(1, bands):
            peer = lax.rem(band + d, bands)
            across.append(
                pltpu.make_async_remote_copy(
                    src_ref=mine.at[peer],
                    dst_ref=got.at[d - 1],
                    send_sem=band_send.at[d - 1],
                    recv_sem=band_recv.at[d - 1],
                    device_id={"band": peer},
                    device_id_type=pl.DeviceIdType.MESH,
                )
            )
        for copy in across:
            copy.start()
        total = mine[band].astype(jnp.float32)
        for d, copy in enumerate(across):
            copy.wait_recv()
            total = total + got[d].astype(jnp.float32)
        out_ref[...] = total.T / nodes_all
        for copy in copies + across:
            copy.wait_send()


def project(filtered, landed, image, slabs, bands):
    nodes, columns = filtered.shape
    middle = bands // 2

    def move(array, pairs):
        perm = []
        for s in range(slabs):
            for a, b in pairs:
                if s % 2:
                    a, b = bands - 1 - a, bands - 1 - b
                perm.append((s * bands + a, s * bands + b))
        return lax.ppermute(array, ("space", "band"), perm)

    rows = [filtered, landed]
    for hop in range(2, middle + 1):
        rows.append(move(rows[-1], [(a, a + 1) for a in range(hop - 1, middle)]))
    images = [image]
    for hop in range(1, bands - middle):
        images.append(move(images[-1], [(a, a - 1) for a in range(middle + 1, bands - hop + 1)]))

    ups, downs = len(rows), len(images)
    states = bands * columns
    share = states // slabs
    dma = pltpu.SemaphoreType.DMA
    narrow = jnp.bfloat16
    chunk = pl.BlockSpec((nodes // EDGE, columns), lambda z: (z, 0))
    early = pl.pallas_call(
        early_kernel,
        grid=(EDGE,),
        in_specs=[chunk] * 3,
        out_specs=pl.BlockSpec((columns, 2 * columns), lambda z: (0, 0)),
        out_shape=jax.ShapeDtypeStruct((columns, 2 * columns), jnp.float32),
        compiler_params=pltpu.CompilerParams(vmem_limit_bytes=VMEM_BYTES),
        cost_estimate=pl.CostEstimate(
            flops=4 * nodes * columns * columns, bytes_accessed=6 * nodes * columns, transcendentals=0
        ),
        name="early_products",
    )(filtered, landed, image)
    projected = pl.pallas_call(
        functools.partial(
            combine_kernel, slabs, bands, ups, downs, FACE * ((EDGE - 1) * slabs + 1)
        ),
        grid=(EDGE,),
        in_specs=[chunk] * (ups + downs)
        + [pl.BlockSpec((columns, 2 * columns), lambda z: (0, 0))],
        out_specs=pl.BlockSpec((columns, share), lambda z: (0, 0)),
        out_shape=jax.ShapeDtypeStruct((columns, share), jnp.float32),
        scratch_shapes=[
            pltpu.VMEM((downs, columns, ups * columns), jnp.float32),
            pltpu.VMEM((states, states), narrow),
            pltpu.VMEM((slabs - 1, share, states), narrow),
            pltpu.VMEM((bands, share, columns), narrow),
            pltpu.VMEM((bands - 1, share, columns), narrow),
            dma((slabs - 1,)),
            dma((slabs - 1,)),
            dma((bands - 1,)),
            dma((bands - 1,)),
        ],
        compiler_params=pltpu.CompilerParams(
            collective_id=2, has_side_effects=True, vmem_limit_bytes=VMEM_BYTES
        ),
        name="combine",
    )(*rows, *images, early)
    return projected


def solution(mesh):
    placed = (P("space", "band"), P("space"), P(), P("space"), P("space", None), P(), P())
    return jax.shard_map(
        functools.partial(local, mesh),
        mesh=mesh,
        in_specs=placed,
        out_specs=(P("space", "band"), P("band", "space")),
        check_vma=False,
    )
```

```python
import functools

import jax
import jax.numpy as jnp
from jax import lax
from jax.experimental import pallas as pl
from jax.experimental.pallas import tpu as pltpu
from jax.sharding import PartitionSpec as P

EDGE = 8
SLAB_XY = 5
STEPS = 4
LANES = 128
SIDE = (EDGE - 1) * SLAB_XY + 1
FACE = SIDE * SIDE
CELLS = SLAB_XY * SLAB_XY
VMEM_BYTES = 58 * 1024 * 1024


def grid_order(connectivity):
    cells = connectivity.reshape(SLAB_XY, SLAB_XY, EDGE, EDGE, EDGE)
    main = cells[..., : EDGE - 1].transpose(2, 0, 3, 1, 4)
    main = main.reshape(EDGE, SLAB_XY, EDGE, SLAB_XY * (EDGE - 1))
    last = cells[:, SLAB_XY - 1, :, :, EDGE - 1].transpose(1, 0, 2)[..., None]
    rows = jnp.concatenate([main, last], axis=3)
    top = rows[:, :, : EDGE - 1].reshape(EDGE, SIDE - 1, SIDE)
    return jnp.concatenate([top, rows[:, SLAB_XY - 1, EDGE - 1 :]], axis=1).reshape(EDGE, FACE)


def sort_kernel(order_ref, states_ref, potential_ref, u_ref, pot_ref):
    z = pl.program_id(0)
    lane = lax.broadcasted_iota(jnp.int32, (FACE, EDGE), 1)
    column = jnp.sum(jnp.where(lane == z, order_ref[...], 0), axis=1, keepdims=True)
    hit = lax.broadcasted_iota(jnp.int32, (FACE, FACE), 1) == column
    picked = jnp.sum(jnp.where(hit, potential_ref[pl.ds(z, 1), :], 0.0), axis=1, keepdims=True)
    pot_ref[pl.ds(z, FACE, stride=EDGE), :] = jnp.broadcast_to(picked, (FACE, LANES))
    one_hot = jnp.where(hit, 1.0, 0.0).astype(jnp.bfloat16)
    rows = jnp.dot(one_hot, states_ref[...], preferred_element_type=jnp.float32)
    for h in range(u_ref.shape[0]):
        u_ref.at[h][pl.ds(z, FACE, stride=EDGE), :] = rows[:, h * LANES : (h + 1) * LANES]


def unsort_kernel(order_ref, f_ref, out_ref, wide):
    z = pl.program_id(0)
    halves = wide.shape[0]

    @pl.when(z == 0)
    def _():
        for h in range(halves):
            wide[h] = f_ref[:, h * LANES : (h + 1) * LANES].astype(jnp.float32)

    row = order_ref[pl.ds(z, 1), :]
    hit = lax.broadcasted_iota(jnp.int32, (FACE, FACE), 0) == row
    one_hot = jnp.where(hit, 1.0, 0.0).astype(jnp.bfloat16)
    plane = jnp.concatenate(
        [wide.at[h][pl.ds(z, FACE, stride=EDGE), :] for h in range(halves)], axis=1
    ).astype(jnp.bfloat16)
    out_ref[...] = jnp.dot(one_hot, plane, preferred_element_type=jnp.float32).astype(jnp.bfloat16)


def filter_kernel(
    count, bands, bounds_ref, scale_ref, u_hbm, pot_ref, matrix_ref, f_ref, w_ref, next_hbm,
    even, odd, acc, send, recv, load_sem, send_sem, recv_sem, hop_send, hop_recv,
):
    halves = acc.shape[0]
    nodes = acc.shape[1]
    me = lax.axis_index("space")
    has_low = me > 0
    has_up = me < count - 1
    barrier = pltpu.get_barrier_semaphore()

    band = lax.axis_index("band")
    swap = lax.rem(me, 2) == 1
    role = jnp.where(swap, bands - 1 - band, band)
    onward = jnp.where(swap, -1, 1)
    gives = role < bands // 2
    takes = (role > 0) & (role <= bands // 2)

    def greet(there, axis, other):
        @pl.when(there)
        def _():
            pl.semaphore_signal(
                barrier, inc=1, device_id={axis: other}, device_id_type=pl.DeviceIdType.MESH
            )

    load = pltpu.make_async_copy(u_hbm, even, load_sem)
    load.start()
    peers = (
        (has_low, "space", me - 1),
        (has_up, "space", me + 1),
        (gives, "band", band + onward),
        (takes, "band", band - onward),
    )
    for peer in peers:
        greet(*peer)
    pl.semaphore_wait(barrier, sum(jnp.where(peer[0], 1, 0) for peer in peers))
    load.wait()

    center = bounds_ref[0]
    inverse = bounds_ref[1]
    plane = lax.broadcasted_iota(jnp.int32, (EDGE, LANES), 0)
    low_w = jnp.where(has_low, 0.5, 1.0).astype(jnp.float32)
    up_w = jnp.where(has_up, 0.5, 1.0).astype(jnp.float32)
    weight = jnp.where(plane == 0, low_w, jnp.where(plane == EDGE - 1, up_w, 1.0))
    chunk = SIDE * EDGE
    weights = jnp.concatenate([weight] * SIDE, axis=0)

    def side_copy(step, h, side):
        return pltpu.make_async_remote_copy(
            src_ref=send.at[step % 2, h, side],
            dst_ref=recv.at[step % 2, h, 1 - side],
            send_sem=send_sem.at[step % 2, h, side],
            recv_sem=recv_sem.at[step % 2, h, 1 - side],
            device_id={"space": me - 1 if side == 0 else me + 1},
            device_id_type=pl.DeviceIdType.MESH,
        )

    def hop(h):
        part = pl.ds(h * LANES, LANES)
        return pltpu.make_async_remote_copy(
            src_ref=f_ref.at[:, part],
            dst_ref=next_hbm.at[:, part],
            send_sem=hop_send.at[h],
            recv_sem=hop_recv.at[h],
            device_id={"band": band + onward},
            device_id_type=pl.DeviceIdType.MESH,
        )

    def start_terms(u, h, shift):
        def body(i, carry):
            rows = pl.ds(pl.multiple_of(i * chunk, EDGE), chunk)
            acc[h, rows, :] = weights * (pot_ref[rows, :] - shift) * u[h, rows, :]
            return carry

        lax.fori_loop(0, SIDE, body, 0)

    def cell_rows(cell, y):
        corner = ((cell // SLAB_XY) * (EDGE - 1) + y) * SIDE + (cell % SLAB_XY) * (EDGE - 1)
        return pl.ds(pl.multiple_of(corner * EDGE, EDGE), EDGE * EDGE)

    def cells(u, h, group):
        blocks = [
            jnp.concatenate(
                [u[h, cell_rows(cell, y), :].astype(jnp.bfloat16) for y in range(EDGE)], axis=0
            )
            for cell in group
        ]
        block = blocks[0] if len(blocks) == 1 else jnp.concatenate(blocks, axis=1)
        product = jnp.dot(matrix_ref[...], block, preferred_element_type=jnp.float32)
        for place, cell in enumerate(group):
            scale = scale_ref[cell]
            for y in range(EDGE):
                part = product[y * EDGE * EDGE : (y + 1) * EDGE * EDGE, place * LANES : (place + 1) * LANES]
                acc[h, cell_rows(cell, y), :] += scale * part

    def all_cells(u, h):
        def body(i, carry):
            cells(u, h, (4 * i, 4 * i + 1))
            cells(u, h, (4 * i + 2, 4 * i + 3))
            return carry

        lax.fori_loop(0, CELLS // 4, body, 0, unroll=2)
        cells(u, h, (CELLS - 1,))

    def ship(step, h):
        for side, there in ((0, has_low), (1, has_up)):
            @pl.when(there)
            def _(side=side):
                rows = pl.ds(side * (EDGE - 1), FACE, stride=EDGE)
                send[step % 2, h, side] = acc.at[h][rows, :].astype(jnp.bfloat16)
                side_copy(step, h, side).start()

    def land(step, h):
        for side, there in ((0, has_low), (1, has_up)):
            @pl.when(there)
            def _(side=side):
                side_copy(step, h, side).wait_send()
                side_copy(step, h, 1 - side).wait_recv()
                rows = pl.ds(side * (EDGE - 1), FACE, stride=EDGE)
                acc.at[h][rows, :] = acc.at[h][rows, :] + recv[step % 2, h, side].astype(jnp.float32)

    def finish(step, h, fresh):
        shift = center if step < STEPS - 1 else 0.0

        def body(i, carry):
            rows = pl.ds(pl.multiple_of(i * chunk, EDGE), chunk)
            total = acc[h, rows, :] * inverse
            if step > 0:
                total = 2.0 * total - fresh[h, rows, :]
            narrow = total.astype(jnp.bfloat16)
            value = narrow.astype(jnp.float32)
            fresh[h, rows, :] = value
            acc[h, rows, :] = weights * (pot_ref[rows, :] - shift) * value
            return carry

        lax.fori_loop(0, SIDE, body, 0)
        if step == STEPS - 1:
            f_ref[:, h * LANES : (h + 1) * LANES] = fresh[h].astype(jnp.bfloat16)

            @pl.when(gives)
            def _():
                hop(h).start()

    fields = (even, odd)
    for h in range(halves):
        start_terms(even, h, center)
        all_cells(even, h)
        ship(0, h)
    for step in range(STEPS):
        fresh = fields[(step + 1) % 2]
        for h in range(halves):
            land(step, h)
            finish(step, h, fresh)
            all_cells(fresh, h)
            if step < STEPS - 1:
                ship(step + 1, h)
            else:
                w_ref[:, h * LANES : (h + 1) * LANES] = acc[h].astype(jnp.bfloat16)
    for h in range(halves):
        @pl.when(gives)
        def _(h=h):
            hop(h).wait_send()

        @pl.when(takes)
        def _(h=h):
            hop(h).wait_recv()


def vmem():
    return pl.BlockSpec(memory_space=pltpu.VMEM)


def smem():
    return pl.BlockSpec(memory_space=pltpu.SMEM)


def local(mesh, states, potential, cell_matrix, cell_scale, connectivity, lower_bound, upper_bound):
    nodes, columns = states.shape
    halves = columns // LANES
    slabs = lax.axis_size("space")
    bands = lax.axis_size("band")
    cell_nodes = cell_matrix.shape[0]
    order = grid_order(connectivity) - jnp.arange(EDGE, dtype=jnp.int32)[:, None] * FACE
    center = (lower_bound + upper_bound) * 0.5
    half_width = (upper_bound - lower_bound) * 0.5
    bounds = jnp.concatenate([center, 1.0 / half_width])

    number = jnp.arange(cell_nodes, dtype=jnp.int32)
    turned = (number % EDGE) * EDGE * EDGE + number // EDGE
    turn = (turned[:, None] == number[None, :]).astype(jnp.bfloat16)
    matrix = jnp.dot(turn, cell_matrix, preferred_element_type=jnp.float32).astype(jnp.bfloat16)
    matrix = jnp.dot(matrix, turn.T, preferred_element_type=jnp.float32).astype(jnp.bfloat16)

    whole = lambda *shape: pl.BlockSpec(shape, lambda z: (0,) * len(shape))
    start, pot = pl.pallas_call(
        sort_kernel,
        grid=(EDGE,),
        in_specs=[
            whole(FACE, EDGE),
            pl.BlockSpec((FACE, columns), lambda z: (z, 0)),
            whole(EDGE, FACE),
        ],
        out_specs=[whole(halves, nodes, LANES), whole(nodes, LANES)],
        out_shape=[
            jax.ShapeDtypeStruct((halves, nodes, LANES), jnp.float32),
            jax.ShapeDtypeStruct((nodes, LANES), jnp.float32),
        ],
        compiler_params=pltpu.CompilerParams(vmem_limit_bytes=VMEM_BYTES),
        name="sort_rows",
    )(order.T, states, potential.reshape(EDGE, FACE))

    dma = pltpu.SemaphoreType.DMA
    field = pltpu.VMEM((halves, nodes, LANES), jnp.float32)
    faces = pltpu.VMEM((2, halves, 2, FACE, LANES), jnp.bfloat16)
    narrow = jax.ShapeDtypeStruct((nodes, columns), jnp.bfloat16)
    filtered, image, landed = pl.pallas_call(
        functools.partial(filter_kernel, slabs, bands),
        in_specs=[smem(), smem(), pl.BlockSpec(memory_space=pl.ANY), vmem(), vmem()],
        out_specs=[vmem(), vmem(), pl.BlockSpec(memory_space=pl.ANY)],
        out_shape=[narrow, narrow, narrow],
        scratch_shapes=[
            field, field, field, faces, faces,
            dma, dma((2, halves, 2)), dma((2, halves, 2)), dma((halves,)), dma((halves,)),
        ],
        compiler_params=pltpu.CompilerParams(
            collective_id=1, has_side_effects=True, vmem_limit_bytes=VMEM_BYTES
        ),
        name="filter_states",
    )(bounds, cell_scale, start, pot, matrix)

    unsort = pl.pallas_call(
        unsort_kernel,
        grid=(EDGE,),
        in_specs=[whole(EDGE, FACE), whole(nodes, columns)],
        out_specs=pl.BlockSpec((FACE, columns), lambda z: (z, 0)),
        out_shape=jax.ShapeDtypeStruct((nodes, columns), jnp.bfloat16),
        scratch_shapes=[field],
        compiler_params=pltpu.CompilerParams(vmem_limit_bytes=VMEM_BYTES),
        cost_estimate=pl.CostEstimate(
            flops=2 * nodes * FACE * columns, bytes_accessed=4 * nodes * columns, transcendentals=0
        ),
        name="unsort_rows",
    )
    return unsort(order, filtered), project(filtered, landed, image, slabs, bands)


def held_by(up, down, bands):
    middle = bands // 2
    first = middle if down else up
    last = middle if up else bands - 1 - down
    return first, last


def early_kernel(f_ref, next_ref, w_ref, out_ref):
    @pl.when(pl.program_id(0) == 0)
    def _():
        out_ref[...] = jnp.zeros_like(out_ref)

    side = jnp.concatenate([f_ref[...], next_ref[...]], axis=1)
    out_ref[...] += lax.dot_general(
        w_ref[...], side, (((0,), (0,)), ((), ())), preferred_element_type=jnp.float32
    )


def combine_kernel(slabs, bands, ups, downs, nodes_all, *refs):
    f_refs, w_refs, early_ref = refs[:ups], refs[ups : ups + downs], refs[ups + downs]
    out_ref, acc, whole, landed, mine, got, send_sem, recv_sem, band_send, band_recv = refs[ups + downs + 1 :]
    step = pl.program_id(0)
    width = acc.shape[1]
    rows = whole.shape[0] // slabs
    me = lax.axis_index("space")
    band = lax.axis_index("band")
    swap = lax.rem(me, 2) == 1
    role = jnp.where(swap, bands - 1 - band, band)
    barrier = pltpu.get_barrier_semaphore()

    @pl.when(step == 0)
    def _():
        for axis, place, count in (("space", me, slabs), ("band", band, bands)):
            for d in range(1, count):
                pl.semaphore_signal(
                    barrier,
                    inc=1,
                    device_id={axis: lax.rem(place + d, count)},
                    device_id_type=pl.DeviceIdType.MESH,
                )
        acc[...] = jnp.zeros_like(acc)
        acc[0, :, : 2 * width] = early_ref[...]

    held = {}
    for r in range(bands):
        for up in range(ups):
            for down in range(downs):
                first, last = held_by(up, down, bands)
                if first <= r <= last:
                    held.setdefault(r, {}).setdefault(down, []).append(up)

    for r, images in held.items():
        @pl.when(role == r)
        def _(images=images):
            for down, fields in images.items():
                begin = 0 if down else 2
                fields = fields[begin:]
                if not fields:
                    continue
                sides = [f_refs[up][...] for up in fields]
                side = sides[0] if len(sides) == 1 else jnp.concatenate(sides, axis=1)
                acc[down, :, begin * width : (begin + len(fields)) * width] += lax.dot_general(
                    w_refs[down][...], side, (((0,), (0,)), ((), ())), preferred_element_type=jnp.float32
                )

    @pl.when(step == pl.num_programs(0) - 1)
    def _():
        whole[...] = jnp.zeros_like(whole)
        for mirrored in range(2):
            for r, images in held.items():
                @pl.when((role == r) & (swap if mirrored else jnp.logical_not(swap)))
                def _(mirrored=mirrored, r=r, images=images):
                    for down, fields in images.items():
                        for up in fields:
                            a, b = r - up, r + down
                            if mirrored:
                                a, b = bands - 1 - a, bands - 1 - b
                            block = acc[down, :, up * width : (up + 1) * width]
                            across, along = pl.ds(b * width, width), pl.ds(a * width, width)
                            whole[across, along] = block.astype(jnp.bfloat16)
                            if a != b:
                                whole[along, across] = block.T.astype(jnp.bfloat16)

        pl.semaphore_wait(barrier, slabs - 1 + bands - 1)
        copies = []
        for d in range(1, slabs):
            peer = lax.rem(me + d, slabs)
            copies.append(
                pltpu.make_async_remote_copy(
                    src_ref=whole.at[pl.ds(pl.multiple_of(peer * rows, rows), rows), :],
                    dst_ref=landed.at[d - 1],
                    send_sem=send_sem.at[d - 1],
                    recv_sem=recv_sem.at[d - 1],
                    device_id={"space": peer},
                    device_id_type=pl.DeviceIdType.MESH,
                )
            )
        for copy in copies:
            copy.start()
        total = whole[pl.ds(pl.multiple_of(me * rows, rows), rows), :].astype(jnp.float32)
        for d, copy in enumerate(copies):
            copy.wait_recv()
            total = total + landed[d].astype(jnp.float32)
        for q in range(bands):
            mine[q] = total[:, q * width : (q + 1) * width].astype(jnp.bfloat16)
        across = []
        for d in range(1, bands):
            peer = lax.rem(band + d, bands)
            across.append(
                pltpu.make_async_remote_copy(
                    src_ref=mine.at[peer],
                    dst_ref=got.at[d - 1],
                    send_sem=band_send.at[d - 1],
                    recv_sem=band_recv.at[d - 1],
                    device_id={"band": peer},
                    device_id_type=pl.DeviceIdType.MESH,
                )
            )
        for copy in across:
            copy.start()
        total = mine[band].astype(jnp.float32)
        for d, copy in enumerate(across):
            copy.wait_recv()
            total = total + got[d].astype(jnp.float32)
        out_ref[...] = total.T / nodes_all
        for copy in copies + across:
            copy.wait_send()


def project(filtered, landed, image, slabs, bands):
    nodes, columns = filtered.shape
    middle = bands // 2

    def move(array, pairs):
        perm = []
        for s in range(slabs):
            for a, b in pairs:
                if s % 2:
                    a, b = bands - 1 - a, bands - 1 - b
                perm.append((s * bands + a, s * bands + b))
        return lax.ppermute(array, ("space", "band"), perm)

    rows = [filtered, landed]
    for hop in range(2, middle + 1):
        rows.append(move(rows[-1], [(a, a + 1) for a in range(hop - 1, middle)]))
    images = [image]
    for hop in range(1, bands - middle):
        images.append(move(images[-1], [(a, a - 1) for a in range(middle + 1, bands - hop + 1)]))

    ups, downs = len(rows), len(images)
    states = bands * columns
    share = states // slabs
    dma = pltpu.SemaphoreType.DMA
    narrow = jnp.bfloat16
    chunk = pl.BlockSpec((nodes // EDGE, columns), lambda z: (z, 0))
    early = pl.pallas_call(
        early_kernel,
        grid=(EDGE,),
        in_specs=[chunk] * 3,
        out_specs=pl.BlockSpec((columns, 2 * columns), lambda z: (0, 0)),
        out_shape=jax.ShapeDtypeStruct((columns, 2 * columns), jnp.float32),
        compiler_params=pltpu.CompilerParams(vmem_limit_bytes=VMEM_BYTES),
        cost_estimate=pl.CostEstimate(
            flops=4 * nodes * columns * columns, bytes_accessed=6 * nodes * columns, transcendentals=0
        ),
        name="early_products",
    )(filtered, landed, image)
    projected = pl.pallas_call(
        functools.partial(
            combine_kernel, slabs, bands, ups, downs, FACE * ((EDGE - 1) * slabs + 1)
        ),
        grid=(EDGE,),
        in_specs=[chunk] * (ups + downs)
        + [pl.BlockSpec((columns, 2 * columns), lambda z: (0, 0))],
        out_specs=pl.BlockSpec((columns, share), lambda z: (0, 0)),
        out_shape=jax.ShapeDtypeStruct((columns, share), jnp.float32),
        scratch_shapes=[
            pltpu.VMEM((downs, columns, ups * columns), jnp.float32),
            pltpu.VMEM((states, states), narrow),
            pltpu.VMEM((slabs - 1, share, states), narrow),
            pltpu.VMEM((bands, share, columns), narrow),
            pltpu.VMEM((bands - 1, share, columns), narrow),
            dma((slabs - 1,)),
            dma((slabs - 1,)),
            dma((bands - 1,)),
            dma((bands - 1,)),
        ],
        compiler_params=pltpu.CompilerParams(
            collective_id=2, has_side_effects=True, vmem_limit_bytes=VMEM_BYTES
        ),
        name="combine",
    )(*rows, *images, early)
    return projected


def solution(mesh):
    placed = (P("space", "band"), P("space"), P(), P("space"), P("space", None), P(), P())
    return jax.shard_map(
        functools.partial(local, mesh),
        mesh=mesh,
        in_specs=placed,
        out_specs=(P("space", "band"), P("band", "space")),
        check_vma=False,
    )
```
